32 devices in a mesh: loop: 16 (over z, x, core), rep: 2 (over y).
Axes of the slice: x: 2, y: 2, z: 4, core: 2. Of those that a mesh axis runs over, the one named last changes fastest.
Arguments:
- features: bfloat16 [4096, 256], P(('loop', 'rep')), may hold values from -6 to 6
- weight: bfloat16 [256, 256], replicated, may hold values from -0.375 to 0.375
- tile_values: bfloat16 [3072, 128, 128], P(('loop', 'rep')), may hold values from -0.375 to 0.375
- tile_coords: int32 [3072, 2], P(('loop', 'rep')), may hold values from 0 to 1
- tile_counts: int32 [32, 8], P(('loop', 'rep')), may hold values from 1 to 12, as said below
Outputs:
- activated: bfloat16 [4096, 256], P(('loop', 'rep'))
The draws below stay inside these ranges and needn't reach their ends.
Inputs may be any that keep to these rules, and one draw needn't show every extreme that they name: `tile_counts`: some list uses all 12 slots at some step; loads differ strongly between lists. `tile_coords`: row block within the group's rows and column block within the slab of that step.
All inputs are finite; a program needn't handle non-finite values.
Results may differ from the reference program's by a relative error of at most 0.0049.
Values may be sent and summed in bfloat16 or wider, within the bound.
No kernel may reach another device: no remote copies, remote signals or barrier semaphores. Data moves between devices by JAX's collectives and lax.ppermute only.
A program may use at most 64 MiB of HBM per device.

```python
import jax
import jax.numpy as jnp
from jax import lax

F = 256
R = 128
TILE = 128
SLOTS = 12
STEPS = 8
BLOCKS = 2
NODES = 4096
N_LOOP = 16
N_REP = 2


def draw_tile_counts(key, part):
    lists = N_LOOP * N_REP
    key_heavy, key_high, key_low, key_peak = jax.random.split(jax.random.fold_in(key, 7), 4)
    heavy = jax.random.randint(key_heavy, (lists, 1), 0, 4) == 0
    high = jax.random.randint(key_high, (lists, STEPS), SLOTS // 2 + 1, SLOTS + 1)
    low = jax.random.randint(key_low, (lists, STEPS), 1, max(2, SLOTS // 3 + 1))
    counts = jnp.where(heavy, high, low).reshape(-1)
    peak = jax.random.randint(key_peak, (), 0, lists * STEPS)
    counts = jnp.where(jnp.arange(lists * STEPS) == peak, SLOTS, counts)
    return counts.reshape(lists, STEPS).astype(jnp.int32)


def with_ends(drawn, key, least, largest):
    extent = drawn.shape
    spot = [jax.random.randint(jax.random.fold_in(key, axis), (), 0, extent[axis]) for axis in range(len(extent))]
    drawn = drawn.at[tuple(spot)].set(least)
    longest = extent.index(max(extent))
    spot[longest] = (spot[longest] + 1) % extent[longest]
    return drawn.at[tuple(spot)].set(largest)


def levels(own_key, shape, shards, least, largest):
    level = 1.0
    for dim, parts in shards:
        steps = jax.random.uniform(jax.random.fold_in(jax.random.fold_in(own_key, 6), dim), (parts,), jnp.float32, least / len(shards), largest / len(shards))
        level = level * jnp.repeat(jnp.exp(steps), shape[dim] // parts).reshape((-1,) + (1,) * (len(shape) - 1 - dim))
    return level


def bell_draw(rng, shape, scale, most, cuts=(), kind=jnp.bfloat16):
    factor_of = levels(rng, shape, cuts, -0.22, 0.18) if cuts else 1.0
    array = jax.random.normal(rng, shape, jnp.float32) * scale * factor_of
    return jnp.minimum(jnp.maximum(array, -most), most).astype(kind)


def setup_inputs(seed: int = 0) -> dict:
    seeds = jax.random.split(jax.random.key(seed), 6)
    return {
        "features": bell_draw(seeds[0], (NODES, F), 1.0, 6.0, ((0, 32),)),
        "weight": bell_draw(seeds[1], (F, F), F ** -0.5, 0.375),
        "tile_values": bell_draw(seeds[2], (N_LOOP * N_REP * STEPS * SLOTS, TILE, TILE), (0.3 / TILE ** 0.5), 0.375, ((0, 32),)),
        "tile_coords": with_ends(jax.random.randint(seeds[3], (N_LOOP * N_REP * STEPS * SLOTS, 2), 0, BLOCKS), jax.random.fold_in(seeds[3], 1), 0, BLOCKS - 1).astype(jnp.int32),
        "tile_counts": draw_tile_counts(jax.random.fold_in(seeds[5], 71), 0),
    }


def reference(features, weight, tile_values, tile_coords, tile_counts):
    width = features.shape[1]
    step_count = N_LOOP // N_REP
    block_count = N_REP * R // TILE
    feature_blocks = features.reshape(N_LOOP * N_REP * R // TILE, TILE, width)
    values = tile_values.reshape(N_LOOP, N_REP, step_count * SLOTS, TILE, TILE)
    coords = tile_coords.reshape(N_LOOP, N_REP, step_count, SLOTS, 2)
    counts = tile_counts.reshape(N_LOOP, N_REP, step_count)

    def group_sum(loop_index):
        def add_rank(running, rep_index):
            tile_block = values[loop_index, rep_index].astype(jnp.float32)
            coord_block = coords[loop_index, rep_index]
            count_row = counts[loop_index, rep_index]
            step_ids = jnp.arange(step_count).astype(jnp.int32)
            slab_ids = jnp.mod(loop_index - step_count * rep_index - step_ids, N_LOOP).astype(jnp.int32)
            columns = (slab_ids[:, None] * block_count + coord_block[:, :, 1]).astype(jnp.int32).reshape(-1)
            pieces = jnp.take(feature_blocks, columns, axis=0).astype(jnp.float32)
            products = jnp.einsum("ktc,kcf->ktf", tile_block, pieces, precision=lax.Precision.HIGHEST)
            live_slot = (jnp.arange(SLOTS)[None, :] < count_row[:, None]).reshape(-1)
            row_ids = coord_block[:, :, 0].reshape(-1)
            placed = ((row_ids[None, :] == jnp.arange(block_count)[:, None]) & live_slot[None, :]).astype(jnp.float32)
            running = running + jnp.einsum("bk,ktf->btf", placed, products, precision=lax.Precision.HIGHEST)
            return running, None

        start = jnp.zeros((block_count, TILE, width), jnp.float32)
        running, unused = lax.scan(add_rank, start, jnp.arange(N_REP).astype(jnp.int32))
        return running.reshape(block_count * TILE, width)

    sums = lax.map(group_sum, jnp.arange(N_LOOP).astype(jnp.int32)).reshape(-1, width)
    aggregated = sums.astype(jnp.bfloat16)
    product = jnp.dot(aggregated, weight, preferred_element_type=jnp.float32)
    return jnp.maximum(product, 0.0).astype(jnp.bfloat16)
```

```python
import functools

import jax
import jax.numpy as jnp
from jax import lax
from jax.experimental import pallas as pl
from jax.experimental.pallas import tpu as pltpu
from jax.sharding import PartitionSpec as P

AXES = ("loop", "rep")
VMEM = pl.BlockSpec(memory_space=pltpu.VMEM)
SMEM = pl.BlockSpec(memory_space=pltpu.SMEM)


def from_behind(x, axis, by):
    count = lax.axis_size(axis)
    return lax.ppermute(x, axis, [(i, (i + by) % count) for i in range(count)])


def ring(features, weight, tile_values, tile_coords, tile_counts):
    rep_size = lax.axis_size("rep")
    loop_size = lax.axis_size("loop")
    step_count = loop_size // rep_size
    tile_size = tile_values.shape[1]
    feat_width = features.shape[1]
    slot_count = tile_values.shape[0] // step_count
    current_slab = lax.all_gather(features, "rep", axis=0, tiled=True)
    block_count = current_slab.shape[0] // tile_size
    values = tile_values.reshape(step_count, slot_count, tile_size, tile_size)
    coords = tile_coords.reshape(step_count, slot_count, 2)
    counts = tile_counts.reshape(step_count)
    rep_rank = lax.axis_index("rep")
    for bit_index in range(rep_size.bit_length() - 1):
        shifted = from_behind(current_slab, "loop", step_count * (1 << bit_index))
        current_slab = jnp.where(rep_rank >> bit_index & 1 == 1, shifted, current_slab)
    running = jnp.zeros((block_count, tile_size, feat_width), jnp.float32)
    for step_index in range(step_count):
        slab_blocks = current_slab.reshape(block_count, tile_size, feat_width)
        pieces = jnp.take(slab_blocks, coords[step_index, :, 1], axis=0)
        products = jnp.einsum(
            "ktc,kcf->ktf", values[step_index], pieces, preferred_element_type=jnp.float32
        )
        live_slot = (jnp.arange(slot_count) < counts[step_index]).astype(jnp.float32)
        running = running.at[coords[step_index, :, 0]].add(products * live_slot[:, None, None])
        if step_index + 1 < step_count:
            current_slab = from_behind(current_slab, "loop", 1)
    summed = lax.psum_scatter(
        running.reshape(block_count * tile_size, feat_width), "rep", scatter_dimension=0, tiled=True
    )
    aggregated = summed.astype(jnp.bfloat16)
    product = jnp.dot(aggregated, weight, preferred_element_type=jnp.float32)
    return jnp.maximum(product, 0.0).astype(jnp.bfloat16)


HELD = 10


def route(planes, move):
    pairs = []
    for z in range(planes):
        for x in range(2):
            for core in range(2):
                for y in range(2):
                    z2, x2, core2, y2 = move(z, x, core, y)
                    pairs.append((((z * 2 + x) * 2 + core) * 2 + y, (((z2 % planes) * 2 + x2) * 2 + core2) * 2 + y2))
    return pairs


def spread(features, planes):
    def send(value, move):
        return lax.ppermute(value, AXES, route(planes, move))

    def sign(y):
        return 1 if y else -1

    own = features
    ahead = send(own, lambda z, x, c, y: (z - sign(y), x, c, y))
    behind = send(own, lambda z, x, c, y: (z + sign(y), x, c, y))
    far = send(own, lambda z, x, c, y: (z + 2, x, c, y))
    near = (lax.axis_index("loop") >> 1 & 1) == lax.axis_index("rep")
    beside = jnp.where(near, jnp.concatenate([own, ahead]), jnp.concatenate([ahead, far]))
    across = jnp.where(near, jnp.concatenate([behind, far]), jnp.concatenate([own, behind]))
    along_y = send(jnp.concatenate([own, behind, far]), lambda z, x, c, y: (z, x, c, 1 - y))
    along_x = send(beside, lambda z, x, c, y: (z, 1 - x, c, y))
    diagonal = send(across, lambda z, x, c, y: (z, 1 - x, c, 1 - y))
    held = [own, ahead, far, along_x, along_y, diagonal]
    other = send(jnp.concatenate(held), lambda z, x, c, y: (z, x, 1 - c, y))
    return held + [other]


def dense_kernel(where, counts, coords, values, out, total):
    step = pl.program_id(0)
    slots = values.shape[0]
    tile = values.shape[1]
    rank = where[8]

    @pl.when(step == 0)
    def _():
        out[...] = jnp.zeros_like(out)

    total[...] = jnp.zeros_like(total)

    def add(slot, carry):
        row = coords[step * slots + slot, 0] ^ rank
        column = coords[step * slots + slot, 1] ^ rank
        spot = row * 2 + column
        total[spot] = total[spot] + values[slot].astype(jnp.float32)
        return carry

    lax.fori_loop(0, counts[0, step], add, 0)
    for row in range(2):
        for column in range(2):
            start = pl.multiple_of((where[step] + column * (HELD // 2)) * tile, tile)
            out[pl.ds(row * tile, tile), pl.ds(start, tile)] = total[row * 2 + column].astype(jnp.bfloat16)


def dense(where, tile_counts, tile_coords, tile_values):
    steps = tile_counts.shape[1]
    slots = tile_values.shape[0] // steps
    tile = tile_values.shape[1]
    return pl.pallas_call(
        dense_kernel,
        grid=(steps,),
        out_shape=jax.ShapeDtypeStruct((2 * tile, 2 * HELD * tile), jnp.bfloat16),
        in_specs=[SMEM, SMEM, SMEM, pl.BlockSpec((slots, tile, tile), lambda i: (i, 0, 0))],
        out_specs=pl.BlockSpec((2 * tile, 2 * HELD * tile), lambda i: (0, 0)),
        scratch_shapes=[pltpu.VMEM((4, tile, tile), jnp.float32)],
        compiler_params=pltpu.CompilerParams(vmem_limit_bytes=24 * 1024 * 1024),
        cost_estimate=pl.CostEstimate(flops=4_000_000, bytes_accessed=6_000_000, transcendentals=0),
    )(where, tile_counts, tile_coords, tile_values)


def product_kernel(row, matrix, *refs):
    out = refs[-1]
    tile = out.shape[0]
    total = jnp.zeros(out.shape, jnp.float32)
    start = 0
    for ref in refs[:-1]:
        depth = ref.shape[0]
        total += jnp.dot(
            matrix[pl.ds(row * tile, tile), pl.ds(start, depth)], ref[...], preferred_element_type=jnp.float32
        )
        start += depth
    out[...] = total.astype(out.dtype)


def products(row, matrix, blocks, dtype):
    tile = matrix.shape[0] // 2
    width = blocks[0].shape[1]
    return pl.pallas_call(
        functools.partial(product_kernel, row),
        out_shape=jax.ShapeDtypeStruct((tile, width), dtype),
        in_specs=[VMEM] * (1 + len(blocks)),
        out_specs=VMEM,
        compiler_params=pltpu.CompilerParams(vmem_limit_bytes=24 * 1024 * 1024),
        cost_estimate=pl.CostEstimate(
            flops=2 * tile * matrix.shape[1] * width, bytes_accessed=2_000_000, transcendentals=0
        ),
    )(matrix, *blocks)


def last_kernel(mine, theirs, weight, out):
    aggregated = (mine[...] + theirs[...].astype(jnp.float32)).astype(jnp.bfloat16)
    product = jnp.dot(aggregated, weight[...], preferred_element_type=jnp.float32)
    out[...] = jnp.maximum(product, 0.0).astype(out.dtype)


def last(mine, theirs, weight):
    return pl.pallas_call(
        last_kernel,
        out_shape=jax.ShapeDtypeStruct(mine.shape, jnp.bfloat16),
        in_specs=[VMEM] * 3,
        out_specs=VMEM,
    )(mine, theirs, weight)


def pairs(features, weight, tile_values, tile_coords, tile_counts):
    planes = lax.axis_size("loop") // 4
    core = lax.axis_index("loop") & 1
    rank = lax.axis_index("rep")
    steps = jnp.arange(8, dtype=jnp.int32)
    odd = steps & 1
    there = odd * (1 - 2 * core)
    k = jnp.where(rank == 0, steps + there, 8 - steps - there) // 2
    where = jnp.where(k % 2 == 0, k // 2, 3 + k // 2) + HELD * odd
    where = jnp.concatenate([where, rank[None]]).astype(jnp.int32)
    matrix = dense(where, tile_counts, tile_coords, tile_values)
    blocks = spread(features, planes)
    theirs = products(1, matrix, blocks, jnp.bfloat16)
    theirs = lax.ppermute(theirs, "rep", [(0, 1), (1, 0)])
    mine = products(0, matrix, blocks, jnp.float32)
    return last(mine, theirs, weight)


def solution(mesh):
    placed = (
        P(AXES, None),
        P(),
        P(AXES, None, None),
        P(AXES, None),
        P(AXES, None),
    )
    local = pairs if dict(mesh.shape) == {"loop": 16, "rep": 2} else ring
    return jax.shard_map(local, mesh=mesh, in_specs=placed, out_specs=P(AXES, None), check_vma=False)
```

```python
import functools

import jax
import jax.numpy as jnp
from jax import lax
from jax.experimental import pallas as pl
from jax.experimental.pallas import tpu as pltpu
from jax.sharding import PartitionSpec as P

AXES = ("loop", "rep")
VMEM = pl.BlockSpec(memory_space=pltpu.VMEM)
SMEM = pl.BlockSpec(memory_space=pltpu.SMEM)


def from_behind(x, axis, by):
    count = lax.axis_size(axis)
    return lax.ppermute(x, axis, [(i, (i + by) % count) for i in range(count)])


def ring(features, weight, tile_values, tile_coords, tile_counts):
    rep_size = lax.axis_size("rep")
    loop_size = lax.axis_size("loop")
    step_count = loop_size // rep_size
    tile_size = tile_values.shape[1]
    feat_width = features.shape[1]
    slot_count = tile_values.shape[0] // step_count
    current_slab = lax.all_gather(features, "rep", axis=0, tiled=True)
    block_count = current_slab.shape[0] // tile_size
    values = tile_values.reshape(step_count, slot_count, tile_size, tile_size)
    coords = tile_coords.reshape(step_count, slot_count, 2)
    counts = tile_counts.reshape(step_count)
    rep_rank = lax.axis_index("rep")
    for bit_index in range(rep_size.bit_length() - 1):
        shifted = from_behind(current_slab, "loop", step_count * (1 << bit_index))
        current_slab = jnp.where(rep_rank >> bit_index & 1 == 1, shifted, current_slab)
    running = jnp.zeros((block_count, tile_size, feat_width), jnp.float32)
    for step_index in range(step_count):
        slab_blocks = current_slab.reshape(block_count, tile_size, feat_width)
        pieces = jnp.take(slab_blocks, coords[step_index, :, 1], axis=0)
        products = jnp.einsum(
            "ktc,kcf->ktf", values[step_index], pieces, preferred_element_type=jnp.float32
        )
        live_slot = (jnp.arange(slot_count) < counts[step_index]).astype(jnp.float32)
        running = running.at[coords[step_index, :, 0]].add(products * live_slot[:, None, None])
        if step_index + 1 < step_count:
            current_slab = from_behind(current_slab, "loop", 1)
    summed = lax.psum_scatter(
        running.reshape(block_count * tile_size, feat_width), "rep", scatter_dimension=0, tiled=True
    )
    aggregated = summed.astype(jnp.bfloat16)
    product = jnp.dot(aggregated, weight, preferred_element_type=jnp.float32)
    return jnp.maximum(product, 0.0).astype(jnp.bfloat16)

HELD = 10
PLACES = (0, 8, 1, 9, 2), (3, 6, 4, 7, 5)
SMALL = 4 * 1024 * 1024
MIDDLE = 24 * 1024 * 1024


def route(planes, move):
    pairs = []
    for z in range(planes):
        for x in range(2):
            for core in range(2):
                for y in range(2):
                    z2, x2, core2, y2 = move(z, x, core, y)
                    pairs.append((((z * 2 + x) * 2 + core) * 2 + y, (((z2 % planes) * 2 + x2) * 2 + core2) * 2 + y2))
    return pairs


def pick_kernel(even, odd, first, second, third, out):
    near = (lax.axis_index("loop") >> 1 & 1) == lax.axis_index("rep")
    rows = first.shape[0]
    refs = (first, second, third)
    for chosen, which in ((jnp.logical_not(near), even), (near, odd)):

        @pl.when(chosen)
        def _(which=which):
            for i, j in enumerate(which):
                out[pl.ds(i * rows, rows)] = refs[j][...]


def pick(even, odd, *blocks):
    rows, width = blocks[0].shape
    return pl.pallas_call(
        functools.partial(pick_kernel, even, odd),
        out_shape=jax.ShapeDtypeStruct((2 * rows, width), blocks[0].dtype),
        in_specs=[VMEM] * 3,
        out_specs=VMEM,
        compiler_params=pltpu.CompilerParams(vmem_limit_bytes=SMALL),
        cost_estimate=pl.CostEstimate(flops=0, bytes_accessed=200_000, transcendentals=0),
    )(*blocks)


def lift_kernel(value, out):
    out[...] = value[...]


def lift(value):
    return pl.pallas_call(
        lift_kernel,
        out_shape=jax.ShapeDtypeStruct(value.shape, value.dtype),
        in_specs=[VMEM],
        out_specs=VMEM,
        compiler_params=pltpu.CompilerParams(vmem_limit_bytes=SMALL),
        cost_estimate=pl.CostEstimate(flops=0, bytes_accessed=200_000, transcendentals=0),
    )(value)


def spread(features, planes, work):
    def send(value, move):
        return lax.ppermute(value, AXES, route(planes, move))

    def sign(y):
        return 1 if y else -1

    own = lift(features)
    far = send(features, lambda z, x, c, y: (z + 2, x, c, y))
    behind = send(features, lambda z, x, c, y: (z + sign(y), x, c, y))
    ahead = send(features, lambda z, x, c, y: (z - sign(y), x, c, y))
    partner = send(features, lambda z, x, c, y: (z, x, c, 1 - y))
    far, own = lax.optimization_barrier((far, own))
    along_y = send(jnp.concatenate([behind, far]), lambda z, x, c, y: (z, x, c, 1 - y))
    behind, partner = lax.optimization_barrier((behind, partner))
    diagonal = send(pick((0, 1), (1, 2), own, behind, far), lambda z, x, c, y: (z, 1 - x, c, 1 - y))
    along_x = send(pick((1, 2), (0, 1), own, ahead, far), lambda z, x, c, y: (z, 1 - x, c, y))
    held = [own, ahead, far, partner, along_y, diagonal, along_x]
    held, work = lax.optimization_barrier((held, work))
    other = send(jnp.concatenate(held), lambda z, x, c, y: (z, x, 1 - c, y))
    return held + [other], work


def dense_kernel(counts, coords, values, out, tiles, total, sems):
    steps = counts.shape[1]
    slots = values.shape[0] // steps
    tile = values.shape[1]
    core = lax.axis_index("loop") & 1
    rank = lax.axis_index("rep")

    def fetch(step):
        span = pl.ds(step * slots, slots)
        return pltpu.make_async_copy(values.at[span], tiles.at[span], sems.at[step])

    for step in range(steps):
        fetch(step).start()
    out[...] = jnp.zeros_like(out)

    def one(step, carry):
        total[...] = jnp.zeros_like(total)
        fetch(step).wait()

        def add(slot, carry):
            row = coords[0, step * slots + slot] ^ rank
            column = coords[1, step * slots + slot] ^ rank
            spot = row * 2 + column
            total[spot] = total[spot] + tiles[step * slots + slot].astype(jnp.float32)
            return carry

        lax.fori_loop(0, counts[0, step], add, 0)
        odd = step & 1
        there = odd * (1 - 2 * core)
        k = jnp.where(rank == 0, step + there, 8 - step - there) >> 1
        for column in range(2):
            place = jnp.int32(0)
            for i, j in enumerate(PLACES[column]):
                place = jnp.where(k == i, j, place)
            start = pl.multiple_of((place + HELD * odd) * tile, tile)
            for row in range(2):
                out[pl.ds(row * tile, tile), pl.ds(start, tile)] = total[row * 2 + column].astype(jnp.bfloat16)
        return carry

    lax.fori_loop(0, steps, one, 0)


def dense(tile_counts, tile_coords, tile_values):
    steps = tile_counts.shape[1]
    tile = tile_values.shape[1]
    return pl.pallas_call(
        dense_kernel,
        out_shape=jax.ShapeDtypeStruct((2 * tile, 2 * HELD * tile), jnp.bfloat16),
        in_specs=[SMEM, SMEM, pl.BlockSpec(memory_space=pltpu.HBM)],
        out_specs=VMEM,
        scratch_shapes=[
            pltpu.VMEM(tile_values.shape, jnp.bfloat16),
            pltpu.VMEM((4, tile, tile), jnp.float32),
            pltpu.SemaphoreType.DMA((steps,)),
        ],
        compiler_params=pltpu.CompilerParams(vmem_limit_bytes=52 * 1024 * 1024),
        cost_estimate=pl.CostEstimate(flops=4_000_000, bytes_accessed=12_000_000, transcendentals=0),
    )(tile_counts, tile_coords.T, tile_values)


def product_kernel(row, matrix, *refs):
    out = refs[-1]
    tile = out.shape[0]
    total = jnp.zeros(out.shape, jnp.float32)
    start = 0
    for ref in refs[:-1]:
        depth = ref.shape[0]
        total += jnp.dot(
            matrix[pl.ds(row * tile, tile), pl.ds(start, depth)], ref[...], preferred_element_type=jnp.float32
        )
        start += depth
    out[...] = total.astype(out.dtype)


def products(row, matrix, blocks, dtype):
    tile = matrix.shape[0] // 2
    width = blocks[0].shape[1]
    return pl.pallas_call(
        functools.partial(product_kernel, row),
        out_shape=jax.ShapeDtypeStruct((tile, width), dtype),
        in_specs=[VMEM] * (1 + len(blocks)),
        out_specs=VMEM,
        compiler_params=pltpu.CompilerParams(vmem_limit_bytes=MIDDLE),
        cost_estimate=pl.CostEstimate(
            flops=2 * tile * matrix.shape[1] * width, bytes_accessed=2_000_000, transcendentals=0
        ),
    )(matrix, *blocks)


def last_kernel(mine, theirs, weight, out):
    aggregated = (mine[...] + theirs[...].astype(jnp.float32)).astype(jnp.bfloat16)
    product = jnp.dot(aggregated, weight[...], preferred_element_type=jnp.float32)
    out[...] = jnp.maximum(product, 0.0).astype(out.dtype)


def last(mine, theirs, weight):
    return pl.pallas_call(
        last_kernel,
        out_shape=jax.ShapeDtypeStruct(mine.shape, jnp.bfloat16),
        in_specs=[VMEM] * 3,
        out_specs=VMEM,
        compiler_params=pltpu.CompilerParams(vmem_limit_bytes=SMALL),
        cost_estimate=pl.CostEstimate(flops=17_000_000, bytes_accessed=400_000, transcendentals=0),
    )(mine, theirs, weight)


def pairs(features, weight, tile_values, tile_coords, tile_counts):
    matrix = dense(tile_counts, tile_coords, tile_values)
    blocks, matrix = spread(features, lax.axis_size("loop") // 4, matrix)
    theirs = products(1, matrix, blocks, jnp.bfloat16)
    theirs = lax.ppermute(theirs, "rep", [(0, 1), (1, 0)])
    mine = products(0, matrix, blocks, jnp.float32)
    return last(mine, theirs, weight)


def solution(mesh):
    placed = (
        P(AXES, None),
        P(),
        P(AXES, None, None),
        P(AXES, None),
        P(AXES, None),
    )
    local = pairs if dict(mesh.shape) == {"loop": 16, "rep": 2} else ring
    return jax.shard_map(local, mesh=mesh, in_specs=placed, out_specs=P(AXES, None), check_vma=False)
```

```python
import functools

import jax
import jax.numpy as jnp
from jax import lax
from jax.experimental import pallas as pl
from jax.experimental.pallas import tpu as pltpu
from jax.sharding import PartitionSpec as P

AXES = ("loop", "rep")
VMEM = pl.BlockSpec(memory_space=pltpu.VMEM)
SMEM = pl.BlockSpec(memory_space=pltpu.SMEM)


def from_behind(x, axis, by):
    count = lax.axis_size(axis)
    return lax.ppermute(x, axis, [(i, (i + by) % count) for i in range(count)])


def ring(features, weight, tile_values, tile_coords, tile_counts):
    rep_size = lax.axis_size("rep")
    loop_size = lax.axis_size("loop")
    step_count = loop_size // rep_size
    tile_size = tile_values.shape[1]
    feat_width = features.shape[1]
    slot_count = tile_values.shape[0] // step_count
    current_slab = lax.all_gather(features, "rep", axis=0, tiled=True)
    block_count = current_slab.shape[0] // tile_size
    values = tile_values.reshape(step_count, slot_count, tile_size, tile_size)
    coords = tile_coords.reshape(step_count, slot_count, 2)
    counts = tile_counts.reshape(step_count)
    rep_rank = lax.axis_index("rep")
    for bit_index in range(rep_size.bit_length() - 1):
        shifted = from_behind(current_slab, "loop", step_count * (1 << bit_index))
        current_slab = jnp.where(rep_rank >> bit_index & 1 == 1, shifted, current_slab)
    running = jnp.zeros((block_count, tile_size, feat_width), jnp.float32)
    for step_index in range(step_count):
        slab_blocks = current_slab.reshape(block_count, tile_size, feat_width)
        pieces = jnp.take(slab_blocks, coords[step_index, :, 1], axis=0)
        products = jnp.einsum(
            "ktc,kcf->ktf", values[step_index], pieces, preferred_element_type=jnp.float32
        )
        live_slot = (jnp.arange(slot_count) < counts[step_index]).astype(jnp.float32)
        running = running.at[coords[step_index, :, 0]].add(products * live_slot[:, None, None])
        if step_index + 1 < step_count:
            current_slab = from_behind(current_slab, "loop", 1)
    summed = lax.psum_scatter(
        running.reshape(block_count * tile_size, feat_width), "rep", scatter_dimension=0, tiled=True
    )
    aggregated = summed.astype(jnp.bfloat16)
    product = jnp.dot(aggregated, weight, preferred_element_type=jnp.float32)
    return jnp.maximum(product, 0.0).astype(jnp.bfloat16)

HELD = 10
SMALL = 4 * 1024 * 1024
MIDDLE = 24 * 1024 * 1024


def route(planes, move):
    pairs = []
    for z in range(planes):
        for x in range(2):
            for core in range(2):
                for y in range(2):
                    z2, x2, core2, y2 = move(z, x, core, y)
                    pairs.append((((z * 2 + x) * 2 + core) * 2 + y, (((z2 % planes) * 2 + x2) * 2 + core2) * 2 + y2))
    return pairs


def pick_kernel(even, odd, *refs):
    out = refs[-1]
    near = (lax.axis_index("loop") >> 1 & 1) == lax.axis_index("rep")
    rows = refs[0].shape[0]
    for chosen, which in ((jnp.logical_not(near), even), (near, odd)):

        @pl.when(chosen)
        def _(which=which):
            for i, j in enumerate(which):
                out[pl.ds(i * rows, rows)] = refs[j][...]


def pick(even, odd, *blocks):
    rows, width = blocks[0].shape
    return pl.pallas_call(
        functools.partial(pick_kernel, even, odd),
        out_shape=jax.ShapeDtypeStruct((len(even) * rows, width), blocks[0].dtype),
        in_specs=[VMEM] * len(blocks),
        out_specs=VMEM,
        compiler_params=pltpu.CompilerParams(vmem_limit_bytes=SMALL),
        cost_estimate=pl.CostEstimate(flops=0, bytes_accessed=200_000, transcendentals=0),
    )(*blocks)


def lift_kernel(*refs):
    for value, out in zip(refs[:3], refs[3:], strict=True):
        out[...] = value[...]


def lift(*values):
    return pl.pallas_call(
        lift_kernel,
        out_shape=[jax.ShapeDtypeStruct(value.shape, value.dtype) for value in values],
        in_specs=[VMEM] * 3,
        out_specs=[VMEM] * 3,
        compiler_params=pltpu.CompilerParams(vmem_limit_bytes=SMALL),
        cost_estimate=pl.CostEstimate(flops=0, bytes_accessed=200_000, transcendentals=0),
    )(*values)


def spread(features, own, planes, matrix):
    def send(value, move):
        return lax.ppermute(value, AXES, route(planes, move))

    def sign(y):
        return 1 if y else -1

    def core(z, x, c, y):
        return z, x, 1 - c, y

    behind = send(features, lambda z, x, c, y: (z + sign(y), x, c, y))
    far = send(features, lambda z, x, c, y: (z + 2, x, c, y))
    behind, late_own = lax.optimization_barrier((behind, own))
    ahead = send(late_own, lambda z, x, c, y: (z - sign(y), x, c, y))
    across = send(pick((0, 1), (1, 2), own, behind, far), lambda z, x, c, y: (z, 1 - x, c, 1 - y))
    along_y = send(pick((0, 1, 2), (0, 1, 2), own, behind, far), lambda z, x, c, y: (z, x, c, 1 - y))
    along_x = send(pick((1, 2), (0, 1), own, ahead, far), lambda z, x, c, y: (z, 1 - x, c, y))
    held = [own, ahead, far, along_y, across, along_x]
    held, matrix = lax.optimization_barrier((held, matrix))
    return held + [send(jnp.concatenate(held), core)], matrix


def dense_kernel(counts, coords, values, out, tiles, total, sems):
    steps = counts.shape[1]
    slots = values.shape[0] // steps
    tile = values.shape[1]
    core = lax.axis_index("loop") & 1
    rank = lax.axis_index("rep")

    def fetch(step):
        span = pl.ds(step * slots, slots)
        return pltpu.make_async_copy(values.at[span], tiles.at[span], sems.at[step])

    for step in range(steps):
        fetch(step).start()
    out[...] = jnp.zeros_like(out)

    def one(step, carry):
        total[...] = jnp.zeros_like(total)
        fetch(step).wait()

        def add(slot, carry):
            row = coords[0, step * slots + slot] ^ rank
            column = coords[1, step * slots + slot] ^ rank
            spot = row * 2 + column
            total[spot] = total[spot] + tiles[step * slots + slot].astype(jnp.float32)
            return carry

        lax.fori_loop(0, counts[0, step], add, 0)
        odd = step & 1
        there = odd * (1 - 2 * core)
        k = jnp.where(rank == 0, step + there, 8 - step - there) >> 1
        half = k >> 1
        places = (jnp.where(k & 1 == 1, 8, 0) + half, jnp.where(k & 1 == 1, 6, 3) + half)
        for column, place in enumerate(places):
            start = pl.multiple_of((place + HELD * odd) * tile, tile)
            for row in range(2):
                out[pl.ds(row * tile, tile), pl.ds(start, tile)] = total[row * 2 + column].astype(jnp.bfloat16)
        return carry

    lax.fori_loop(0, steps, one, 0)


def dense(tile_counts, tile_coords, tile_values):
    steps = tile_counts.shape[1]
    tile = tile_values.shape[1]
    return pl.pallas_call(
        dense_kernel,
        out_shape=jax.ShapeDtypeStruct((2 * tile, 2 * HELD * tile), jnp.bfloat16),
        in_specs=[SMEM, SMEM, pl.BlockSpec(memory_space=pltpu.HBM)],
        out_specs=VMEM,
        scratch_shapes=[
            pltpu.VMEM(tile_values.shape, jnp.bfloat16),
            pltpu.VMEM((4, tile, tile), jnp.float32),
            pltpu.SemaphoreType.DMA((steps,)),
        ],
        compiler_params=pltpu.CompilerParams(vmem_limit_bytes=52 * 1024 * 1024),
        cost_estimate=pl.CostEstimate(flops=4_000_000, bytes_accessed=12_000_000, transcendentals=0),
    )(tile_counts, tile_coords, tile_values)


def product_kernel(row, matrix, *refs):
    out = refs[-1]
    tile = out.shape[0]
    total = jnp.zeros(out.shape, jnp.float32)
    start = 0
    for ref in refs[:-1]:
        depth = ref.shape[0]
        total += jnp.dot(
            matrix[pl.ds(row * tile, tile), pl.ds(start, depth)], ref[...], preferred_element_type=jnp.float32
        )
        start += depth
    out[...] = total.astype(out.dtype)


def products(row, matrix, blocks, dtype):
    tile = matrix.shape[0] // 2
    width = blocks[0].shape[1]
    return pl.pallas_call(
        functools.partial(product_kernel, row),
        out_shape=jax.ShapeDtypeStruct((tile, width), dtype),
        in_specs=[VMEM] * (1 + len(blocks)),
        out_specs=VMEM,
        compiler_params=pltpu.CompilerParams(vmem_limit_bytes=MIDDLE),
        cost_estimate=pl.CostEstimate(
            flops=2 * tile * matrix.shape[1] * width, bytes_accessed=2_000_000, transcendentals=0
        ),
    )(matrix, *blocks)


def last_kernel(mine, theirs, weight, out):
    aggregated = (mine[...] + theirs[...].astype(jnp.float32)).astype(jnp.bfloat16)
    product = jnp.dot(aggregated, weight[...], preferred_element_type=jnp.float32)
    out[...] = jnp.maximum(product, 0.0).astype(out.dtype)


def last(mine, theirs, weight):
    return pl.pallas_call(
        last_kernel,
        out_shape=jax.ShapeDtypeStruct(mine.shape, jnp.bfloat16),
        in_specs=[VMEM] * 3,
        out_specs=VMEM,
        compiler_params=pltpu.CompilerParams(vmem_limit_bytes=SMALL),
        cost_estimate=pl.CostEstimate(flops=17_000_000, bytes_accessed=400_000, transcendentals=0),
    )(mine, theirs, weight)


def pairs(features, weight, tile_values, tile_coords, tile_counts):
    own, tile_counts, tile_coords = lift(features, tile_counts, tile_coords.T)
    matrix = dense(tile_counts, tile_coords, tile_values)
    blocks, matrix = spread(features, own, lax.axis_size("loop") // 4, matrix)
    theirs = products(1, matrix, blocks, jnp.bfloat16)
    theirs = lax.ppermute(theirs, "rep", [(0, 1), (1, 0)])
    mine = products(0, matrix, blocks, jnp.float32)
    return last(mine, theirs, weight)


def solution(mesh):
    placed = (
        P(AXES, None),
        P(),
        P(AXES, None, None),
        P(AXES, None),
        P(AXES, None),
    )
    local = pairs if dict(mesh.shape) == {"loop": 16, "rep": 2} else ring
    return jax.shard_map(local, mesh=mesh, in_specs=placed, out_specs=P(AXES, None), check_vma=False)
```

```python
import functools

import jax
import jax.numpy as jnp
from jax import lax
from jax.experimental import pallas as pl
from jax.experimental.pallas import tpu as pltpu
from jax.sharding import PartitionSpec as P

AXES = ("loop", "rep")
VMEM = pl.BlockSpec(memory_space=pltpu.VMEM)
SMEM = pl.BlockSpec(memory_space=pltpu.SMEM)


def from_behind(x, axis, by):
    count = lax.axis_size(axis)
    return lax.ppermute(x, axis, [(i, (i + by) % count) for i in range(count)])


def ring(features, weight, tile_values, tile_coords, tile_counts):
    rep_size = lax.axis_size("rep")
    loop_size = lax.axis_size("loop")
    step_count = loop_size // rep_size
    tile_size = tile_values.shape[1]
    feat_width = features.shape[1]
    slot_count = tile_values.shape[0] // step_count
    current_slab = lax.all_gather(features, "rep", axis=0, tiled=True)
    block_count = current_slab.shape[0] // tile_size
    values = tile_values.reshape(step_count, slot_count, tile_size, tile_size)
    coords = tile_coords.reshape(step_count, slot_count, 2)
    counts = tile_counts.reshape(step_count)
    rep_rank = lax.axis_index("rep")
    for bit_index in range(rep_size.bit_length() - 1):
        shifted = from_behind(current_slab, "loop", step_count * (1 << bit_index))
        current_slab = jnp.where(rep_rank >> bit_index & 1 == 1, shifted, current_slab)
    running = jnp.zeros((block_count, tile_size, feat_width), jnp.float32)
    for step_index in range(step_count):
        slab_blocks = current_slab.reshape(block_count, tile_size, feat_width)
        pieces = jnp.take(slab_blocks, coords[step_index, :, 1], axis=0)
        products = jnp.einsum(
            "ktc,kcf->ktf", values[step_index], pieces, preferred_element_type=jnp.float32
        )
        live_slot = (jnp.arange(slot_count) < counts[step_index]).astype(jnp.float32)
        running = running.at[coords[step_index, :, 0]].add(products * live_slot[:, None, None])
        if step_index + 1 < step_count:
            current_slab = from_behind(current_slab, "loop", 1)
    summed = lax.psum_scatter(
        running.reshape(block_count * tile_size, feat_width), "rep", scatter_dimension=0, tiled=True
    )
    aggregated = summed.astype(jnp.bfloat16)
    product = jnp.dot(aggregated, weight, preferred_element_type=jnp.float32)
    return jnp.maximum(product, 0.0).astype(jnp.bfloat16)

HELD = 12
SENT = 10
SMALL = 4 * 1024 * 1024
MIDDLE = 24 * 1024 * 1024


def route(planes, move):
    pairs = []
    for z in range(planes):
        for x in range(2):
            for core in range(2):
                for y in range(2):
                    z2, x2, core2, y2 = move(z, x, core, y)
                    pairs.append((((z * 2 + x) * 2 + core) * 2 + y, (((z2 % planes) * 2 + x2) * 2 + core2) * 2 + y2))
    return pairs


def pick_kernel(even, odd, *refs):
    out = refs[-1]
    near = (lax.axis_index("loop") >> 1 & 1) == lax.axis_index("rep")
    for chosen, which in ((jnp.logical_not(near), even), (near, odd)):

        @pl.when(chosen)
        def _(which=which):
            start = 0
            for j in which:
                rows = refs[j].shape[0]
                out[pl.ds(start, rows)] = refs[j][...]
                start += rows


def pick(even, odd, *blocks):
    width = blocks[0].shape[1]
    rows = sum(blocks[j].shape[0] for j in even)
    return pl.pallas_call(
        functools.partial(pick_kernel, even, odd),
        out_shape=jax.ShapeDtypeStruct((rows, width), blocks[0].dtype),
        in_specs=[VMEM] * len(blocks),
        out_specs=VMEM,
        compiler_params=pltpu.CompilerParams(vmem_limit_bytes=SMALL),
        cost_estimate=pl.CostEstimate(flops=0, bytes_accessed=200_000, transcendentals=0),
    )(*blocks)


def pair_kernel(own, mate, mark, out):
    core = lax.axis_index("loop") & 1
    rows = own.shape[0]
    out[pl.ds(pl.multiple_of(core * rows, rows), rows)] = own[...]
    out[pl.ds(pl.multiple_of((1 - core) * rows, rows), rows)] = mate[...]


def pair(own, mate, mark):
    return pl.pallas_call(
        pair_kernel,
        out_shape=jax.ShapeDtypeStruct((2 * own.shape[0], own.shape[1]), own.dtype),
        in_specs=[VMEM] * 3,
        out_specs=VMEM,
        compiler_params=pltpu.CompilerParams(vmem_limit_bytes=SMALL),
        cost_estimate=pl.CostEstimate(flops=0, bytes_accessed=200_000, transcendentals=0),
    )(own, mate, mark)


def mark_kernel(*refs):
    refs[-1][...] = refs[0][pl.ds(0, 16), pl.ds(0, 128)]


def mark(cost, *values):
    return pl.pallas_call(
        mark_kernel,
        out_shape=jax.ShapeDtypeStruct((16, 128), values[0].dtype),
        in_specs=[VMEM] * len(values),
        out_specs=VMEM,
        compiler_params=pltpu.CompilerParams(vmem_limit_bytes=SMALL),
        cost_estimate=pl.CostEstimate(flops=cost, bytes_accessed=4096, transcendentals=0),
    )(*values)


def pack_kernel(*refs):
    out = refs[-1]
    start = 0
    for block in refs[:-2]:
        out[pl.ds(start, block.shape[0])] = block[...]
        start += block.shape[0]


def pack(blocks, mark):
    rows = sum(block.shape[0] for block in blocks)
    return pl.pallas_call(
        pack_kernel,
        out_shape=jax.ShapeDtypeStruct((rows, blocks[0].shape[1]), blocks[0].dtype),
        in_specs=[VMEM] * (len(blocks) + 1),
        out_specs=VMEM,
        compiler_params=pltpu.CompilerParams(vmem_limit_bytes=SMALL),
        cost_estimate=pl.CostEstimate(flops=0, bytes_accessed=1_300_000, transcendentals=0),
    )(*blocks, mark)


def lift_kernel(*refs):
    for value, out in zip(refs[:3], refs[3:], strict=True):
        out[...] = value[...]


def lift(*values):
    return pl.pallas_call(
        lift_kernel,
        out_shape=[jax.ShapeDtypeStruct(value.shape, value.dtype) for value in values],
        in_specs=[VMEM] * 3,
        out_specs=[VMEM] * 3,
        compiler_params=pltpu.CompilerParams(vmem_limit_bytes=SMALL),
        cost_estimate=pl.CostEstimate(flops=0, bytes_accessed=200_000, transcendentals=0),
    )(*values)


def spread(features, own, planes, counts, coords, tile_values):
    def send(value, move):
        return lax.ppermute(value, AXES, route(planes, move))

    def sign(y):
        return 1 if y else -1

    def core(z, x, c, y):
        return z, x, 1 - c, y

    behind = send(features, lambda z, x, c, y: (z + sign(y), x, c, y))
    far = send(features, lambda z, x, c, y: (z + 2, x, c, y))
    mate = send(features, core)
    both = pair(own, mate, mark(4_000_000_000, behind))
    ahead = send(both, lambda z, x, c, y: (z - sign(y), x, c, y) if c else (z, x, c, 1 - y))
    along_y = send(pick((0, 1), (0, 1), behind, far), lambda z, x, c, y: (z, x, c, 1 - y))
    across = send(pick((0, 1), (1, 2), own, behind, far), lambda z, x, c, y: (z, 1 - x, c, 1 - y))
    along_x = send(pick((1,), (0,), own, far), lambda z, x, c, y: (z, 1 - x, c, y))
    ahead, counts, coords = lax.optimization_barrier((ahead, counts, coords))
    matrix = dense(counts, coords, tile_values)
    beside = send(ahead, lambda z, x, c, y: (z, 1 - x, c, y) if c else (z, x, c, y))
    sent = [far, along_y, across, along_x, ahead, beside]
    held = [own, mate] + sent
    arrived = mark(4_000_000_000, along_y, across, along_x, matrix)
    sent, held, matrix = lax.optimization_barrier((sent, held, matrix))
    other = send(pack(sent, arrived), core)
    return [other], matrix, first_products(matrix, held)


def dense_kernel(counts, coords, values, out, tiles, total, sems):
    steps = counts.shape[1]
    slots = values.shape[0] // steps
    tile = values.shape[1]
    core = lax.axis_index("loop") & 1
    rank = lax.axis_index("rep")

    def fetch(step):
        span = pl.ds(step * slots, slots)
        return pltpu.make_async_copy(values.at[span], tiles.at[span], sems.at[step])

    for step in range(steps):
        fetch(step).start()
    out[...] = jnp.zeros_like(out)

    def one(step, carry):
        total[...] = jnp.zeros_like(total)
        fetch(step).wait()

        def add(slot, carry):
            row = coords[0, step * slots + slot] ^ rank
            column = coords[1, step * slots + slot] ^ rank
            spot = row * 2 + column
            total[spot] = total[spot] + tiles[step * slots + slot].astype(jnp.float32)
            return carry

        lax.fori_loop(0, counts[0, step], add, 0)
        odd = step & 1
        there = odd * (1 - 2 * core)
        k = jnp.where(rank == 0, step + there, 8 - step - there) >> 1
        half = k >> 1
        parity = core ^ odd
        other = 1 - core
        near = (lax.axis_index("loop") >> 1 & 1) == rank
        paired = 8 + parity + SENT * other
        straight = jnp.where(k == 2, paired, jnp.where(k == 0, odd, 2 + SENT * odd))
        beside = jnp.where((k == 1) == near, paired + 2, 7 + SENT * odd)
        turned = jnp.where(k == 0, 8 + parity + SENT * core, 2 + half + SENT * odd)
        places = (
            jnp.where(k & 1 == 1, beside, straight),
            jnp.where(k & 1 == 1, 5 + half + SENT * odd, turned),
        )
        for column, place in enumerate(places):
            start = pl.multiple_of(place * tile, tile)
            for row in range(2):
                out[pl.ds(row * tile, tile), pl.ds(start, tile)] = total[row * 2 + column].astype(jnp.bfloat16)
        return carry

    lax.fori_loop(0, steps, one, 0)


def dense(tile_counts, tile_coords, tile_values):
    steps = tile_counts.shape[1]
    tile = tile_values.shape[1]
    return pl.pallas_call(
        dense_kernel,
        out_shape=jax.ShapeDtypeStruct((2 * tile, (HELD + SENT) * tile), jnp.bfloat16),
        in_specs=[SMEM, SMEM, pl.BlockSpec(memory_space=pltpu.HBM)],
        out_specs=VMEM,
        scratch_shapes=[
            pltpu.VMEM(tile_values.shape, jnp.bfloat16),
            pltpu.VMEM((4, tile, tile), jnp.float32),
            pltpu.SemaphoreType.DMA((steps,)),
        ],
        compiler_params=pltpu.CompilerParams(vmem_limit_bytes=52 * 1024 * 1024),
        cost_estimate=pl.CostEstimate(flops=4_000_000, bytes_accessed=12_000_000, transcendentals=0),
    )(tile_counts, tile_coords, tile_values)


def dots(rows, start, matrix, blocks, total):
    for block in blocks:
        depth = block.shape[0]
        part = matrix[rows, pl.ds(start, depth)]
        total += jnp.dot(part, block[...], preferred_element_type=jnp.float32)
        start += depth
    return total


def first_kernel(matrix, *refs):
    out = refs[-1]
    out[...] = dots(pl.ds(0, out.shape[0]), 0, matrix, refs[:-1], jnp.zeros(out.shape, jnp.float32))


def first_products(matrix, blocks):
    width = blocks[0].shape[1]
    return pl.pallas_call(
        first_kernel,
        out_shape=jax.ShapeDtypeStruct((matrix.shape[0], width), jnp.float32),
        in_specs=[VMEM] * (1 + len(blocks)),
        out_specs=VMEM,
        compiler_params=pltpu.CompilerParams(vmem_limit_bytes=MIDDLE),
        cost_estimate=pl.CostEstimate(flops=268_000_000, bytes_accessed=2_000_000, transcendentals=0),
    )(matrix, *blocks)


def product_kernel(row, matrix, sums, *refs):
    out = refs[-1]
    tile = out.shape[0]
    rows = pl.ds(row * tile, tile)
    out[...] = dots(rows, HELD * tile, matrix, refs[:-1], sums[rows]).astype(out.dtype)


def products(row, matrix, sums, blocks, dtype):
    tile = matrix.shape[0] // 2
    width = blocks[0].shape[1]
    return pl.pallas_call(
        functools.partial(product_kernel, row),
        out_shape=jax.ShapeDtypeStruct((tile, width), dtype),
        in_specs=[VMEM] * (2 + len(blocks)),
        out_specs=VMEM,
        compiler_params=pltpu.CompilerParams(vmem_limit_bytes=MIDDLE),
        cost_estimate=pl.CostEstimate(flops=100_000_000, bytes_accessed=2_000_000, transcendentals=0),
    )(matrix, sums, *blocks)


def last_kernel(mine, theirs, weight, out):
    aggregated = (mine[...] + theirs[...].astype(jnp.float32)).astype(jnp.bfloat16)
    product = jnp.dot(aggregated, weight[...], preferred_element_type=jnp.float32)
    out[...] = jnp.maximum(product, 0.0).astype(out.dtype)


def last(mine, theirs, weight):
    return pl.pallas_call(
        last_kernel,
        out_shape=jax.ShapeDtypeStruct(mine.shape, jnp.bfloat16),
        in_specs=[VMEM] * 3,
        out_specs=VMEM,
        compiler_params=pltpu.CompilerParams(vmem_limit_bytes=SMALL),
        cost_estimate=pl.CostEstimate(flops=17_000_000, bytes_accessed=400_000, transcendentals=0),
    )(mine, theirs, weight)


def pairs(features, weight, tile_values, tile_coords, tile_counts):
    own, tile_counts, tile_coords = lift(features, tile_counts, tile_coords.T)
    planes = lax.axis_size("loop") // 4
    blocks, matrix, sums = spread(features, own, planes, tile_counts, tile_coords, tile_values)
    theirs = products(1, matrix, sums, blocks, jnp.bfloat16)
    theirs = lax.ppermute(theirs, "rep", [(0, 1), (1, 0)])
    mine = products(0, matrix, sums, blocks, jnp.float32)
    return last(mine, theirs, weight)


def solution(mesh):
    placed = (
        P(AXES, None),
        P(),
        P(AXES, None, None),
        P(AXES, None),
        P(AXES, None),
    )
    local = pairs if dict(mesh.shape) == {"loop": 16, "rep": 2} else ring
    return jax.shard_map(local, mesh=mesh, in_specs=placed, out_specs=P(AXES, None), check_vma=False)
```

```python
import functools

import jax
import jax.numpy as jnp
from jax import lax
from jax.experimental import pallas as pl
from jax.experimental.pallas import tpu as pltpu
from jax.sharding import PartitionSpec as P

AXES = ("loop", "rep")
VMEM = pl.BlockSpec(memory_space=pltpu.VMEM)
SMEM = pl.BlockSpec(memory_space=pltpu.SMEM)


def from_behind(x, axis, by):
    count = lax.axis_size(axis)
    return lax.ppermute(x, axis, [(i, (i + by) % count) for i in range(count)])


def ring(features, weight, tile_values, tile_coords, tile_counts):
    rep_size = lax.axis_size("rep")
    loop_size = lax.axis_size("loop")
    step_count = loop_size // rep_size
    tile_size = tile_values.shape[1]
    feat_width = features.shape[1]
    slot_count = tile_values.shape[0] // step_count
    current_slab = lax.all_gather(features, "rep", axis=0, tiled=True)
    block_count = current_slab.shape[0] // tile_size
    values = tile_values.reshape(step_count, slot_count, tile_size, tile_size)
    coords = tile_coords.reshape(step_count, slot_count, 2)
    counts = tile_counts.reshape(step_count)
    rep_rank = lax.axis_index("rep")
    for bit_index in range(rep_size.bit_length() - 1):
        shifted = from_behind(current_slab, "loop", step_count * (1 << bit_index))
        current_slab = jnp.where(rep_rank >> bit_index & 1 == 1, shifted, current_slab)
    running = jnp.zeros((block_count, tile_size, feat_width), jnp.float32)
    for step_index in range(step_count):
        slab_blocks = current_slab.reshape(block_count, tile_size, feat_width)
        pieces = jnp.take(slab_blocks, coords[step_index, :, 1], axis=0)
        products = jnp.einsum(
            "ktc,kcf->ktf", values[step_index], pieces, preferred_element_type=jnp.float32
        )
        live_slot = (jnp.arange(slot_count) < counts[step_index]).astype(jnp.float32)
        running = running.at[coords[step_index, :, 0]].add(products * live_slot[:, None, None])
        if step_index + 1 < step_count:
            current_slab = from_behind(current_slab, "loop", 1)
    summed = lax.psum_scatter(
        running.reshape(block_count * tile_size, feat_width), "rep", scatter_dimension=0, tiled=True
    )
    aggregated = summed.astype(jnp.bfloat16)
    product = jnp.dot(aggregated, weight, preferred_element_type=jnp.float32)
    return jnp.maximum(product, 0.0).astype(jnp.bfloat16)

HELD = 11
SMALL = 4 * 1024 * 1024
MIDDLE = 24 * 1024 * 1024


def route(planes, move):
    pairs = []
    for z in range(planes):
        for x in range(2):
            for core in range(2):
                for y in range(2):
                    z2, x2, core2, y2 = move(z, x, core, y)
                    pairs.append((((z * 2 + x) * 2 + core) * 2 + y, (((z2 % planes) * 2 + x2) * 2 + core2) * 2 + y2))
    return pairs


def pick_kernel(even, odd, *refs):
    out = refs[-1]
    near = (lax.axis_index("loop") >> 1 & 1) == lax.axis_index("rep")
    for chosen, which in ((jnp.logical_not(near), even), (near, odd)):

        @pl.when(chosen)
        def _(which=which):
            start = 0
            for j in which:
                rows = refs[j].shape[0]
                out[pl.ds(start, rows)] = refs[j][...]
                start += rows


def pick(even, odd, *blocks):
    width = blocks[0].shape[1]
    rows = sum(blocks[j].shape[0] for j in even)
    return pl.pallas_call(
        functools.partial(pick_kernel, even, odd),
        out_shape=jax.ShapeDtypeStruct((rows, width), blocks[0].dtype),
        in_specs=[VMEM] * len(blocks),
        out_specs=VMEM,
        compiler_params=pltpu.CompilerParams(vmem_limit_bytes=SMALL),
        cost_estimate=pl.CostEstimate(flops=0, bytes_accessed=200_000, transcendentals=0),
    )(*blocks)


def pair_kernel(value, mate, mark, matrix, both, own):
    core = lax.axis_index("loop") & 1
    rows = value.shape[0]
    both[pl.ds(pl.multiple_of(core * rows, rows), rows)] = value[...]
    both[pl.ds(pl.multiple_of((1 - core) * rows, rows), rows)] = mate[...]
    own[...] = value[...]


def pair(value, mate, mark, matrix):
    rows, width = value.shape
    return pl.pallas_call(
        pair_kernel,
        out_shape=[jax.ShapeDtypeStruct((n * rows, width), value.dtype) for n in (2, 1)],
        in_specs=[VMEM] * 4,
        out_specs=[VMEM] * 2,
        compiler_params=pltpu.CompilerParams(vmem_limit_bytes=SMALL),
        cost_estimate=pl.CostEstimate(flops=0, bytes_accessed=200_000, transcendentals=0),
    )(value, mate, mark, matrix)


def pause_kernel(out):
    out[...] = jnp.zeros_like(out)


def pause(cost):
    return pl.pallas_call(
        pause_kernel,
        out_shape=jax.ShapeDtypeStruct((16, 128), jnp.bfloat16),
        out_specs=VMEM,
        compiler_params=pltpu.CompilerParams(vmem_limit_bytes=SMALL),
        cost_estimate=pl.CostEstimate(flops=cost, bytes_accessed=4096, transcendentals=0),
    )()


def mark_kernel(*refs):
    refs[-1][...] = refs[0][pl.ds(0, 16), pl.ds(0, 128)]


def mark(cost, *values):
    return pl.pallas_call(
        mark_kernel,
        out_shape=jax.ShapeDtypeStruct((16, 128), values[0].dtype),
        in_specs=[VMEM] * len(values),
        out_specs=VMEM,
        compiler_params=pltpu.CompilerParams(vmem_limit_bytes=SMALL),
        cost_estimate=pl.CostEstimate(flops=cost, bytes_accessed=4096, transcendentals=0),
    )(*values)


def spread(features, planes, counts, coords, tile_values):
    def send(value, move):
        return lax.ppermute(value, AXES, route(planes, move))

    def sign(y):
        return 1 if y else -1

    def core(z, x, c, y):
        return z, x, 1 - c, y

    behind = send(features, lambda z, x, c, y: (z + sign(y), x, c, y))
    far = send(features, lambda z, x, c, y: (z + 2, x, c, y))
    mate = send(features, core)
    kept, given = dense(pause(1_000_000_000), counts, coords, tile_values)
    taken = send(given, core)
    both, own = pair(features, mate, mark(500_000_000, behind), kept)
    ahead = send(both, lambda z, x, c, y: (z - sign(y), x, c, y) if c else (z, x, c, 1 - y))
    ready = mark(40_000_000_000, far)
    done = mark(1, taken)
    along_y = send(pick((0, 1), (0, 1), behind, far, done, ready), lambda z, x, c, y: (z, x, c, 1 - y))
    across = send(pick((0, 1), (1, 2), own, behind, far, done, ready), lambda z, x, c, y: (z, 1 - x, c, 1 - y))
    along_x = send(pick((1,), (0,), own, far, done, ready), lambda z, x, c, y: (z, 1 - x, c, y))
    beside = send(ahead, lambda z, x, c, y: (z, 1 - x, c, y) if c else (z, x, c, y))
    arrived = mark(4_000_000_000, along_y, across, along_x)
    held = [own, far, along_y, across, along_x, ahead, beside]
    other = send(products(taken, held, arrived, jnp.bfloat16), core)
    mine = products(kept, held, arrived, jnp.float32)
    theirs = send(partner_sum(mine, other), lambda z, x, c, y: (z, x, c, 1 - y))
    return mine, other, theirs


def dense_kernel(mark, counts, coords, values, kept, given, total):
    steps = counts.shape[1]
    slots = values.shape[0] // steps
    tile = values.shape[1]
    core = lax.axis_index("loop") & 1
    rank = lax.axis_index("rep")
    near = (lax.axis_index("loop") >> 1 & 1) == rank
    kept[...] = jnp.zeros_like(kept)
    given[...] = jnp.zeros_like(given)

    def one(step, carry):
        total[...] = jnp.zeros_like(total)

        def add(slot, carry):
            row = coords[0, step * slots + slot] ^ rank
            column = coords[1, step * slots + slot] ^ rank
            spot = row * 2 + column
            total[spot] = total[spot] + values[step * slots + slot].astype(jnp.float32)
            return carry

        lax.fori_loop(0, counts[0, step], add, 0)
        odd = step & 1
        there = odd * (1 - 2 * core)
        k = jnp.where(rank == 0, step + there, steps - step - there) >> 1
        half = k >> 1
        parity = core ^ odd
        turned = k & 1 == 1
        paired = (k == 1) == near
        straight = jnp.where(k == 2, 7 + parity, half >> 1)
        homes = (
            jnp.where(jnp.where(turned, paired, k == 2), 1, parity),
            jnp.where(k == 0, 0, parity),
        )
        places = (
            jnp.where(turned, jnp.where(paired, 9 + parity, 6), straight),
            jnp.where(turned, 4 + half, jnp.where(k == 0, 7 + parity, 1 + half)),
        )
        for column in range(2):
            start = pl.multiple_of(places[column] * tile, tile)
            for out, here in ((kept, homes[column] == core), (given, homes[column] != core)):

                @pl.when(here)
                def _(out=out, column=column, start=start):
                    for row in range(2):
                        piece = total[row * 2 + column].astype(jnp.bfloat16)
                        out[pl.ds(row * tile, tile), pl.ds(start, tile)] = piece

        return carry

    lax.fori_loop(0, steps, one, 0)


def dense(mark, tile_counts, tile_coords, tile_values):
    tile = tile_values.shape[1]
    return pl.pallas_call(
        dense_kernel,
        out_shape=[jax.ShapeDtypeStruct((2 * tile, HELD * tile), jnp.bfloat16)] * 2,
        in_specs=[VMEM, SMEM, SMEM, VMEM],
        out_specs=[VMEM, VMEM],
        scratch_shapes=[pltpu.VMEM((4, tile, tile), jnp.float32)],
        compiler_params=pltpu.CompilerParams(vmem_limit_bytes=MIDDLE),
        cost_estimate=pl.CostEstimate(flops=1, bytes_accessed=1, transcendentals=0),
    )(mark, tile_counts, tile_coords, tile_values)


def product_kernel(matrix, mark, *refs):
    out = refs[-1]
    total = jnp.zeros(out.shape, jnp.float32)
    start = 0
    for block in refs[:-1]:
        depth = block.shape[0]
        total += jnp.dot(matrix[:, pl.ds(start, depth)], block[...], preferred_element_type=jnp.float32)
        start += depth
    out[...] = total.astype(out.dtype)


def products(matrix, blocks, mark, dtype):
    rows = matrix.shape[0]
    width = blocks[0].shape[1]
    return pl.pallas_call(
        product_kernel,
        out_shape=jax.ShapeDtypeStruct((rows, width), dtype),
        in_specs=[VMEM] * (2 + len(blocks)),
        out_specs=VMEM,
        compiler_params=pltpu.CompilerParams(vmem_limit_bytes=MIDDLE),
        cost_estimate=pl.CostEstimate(flops=168_000_000, bytes_accessed=1_000_000, transcendentals=0),
    )(matrix, mark, *blocks)


def sum_kernel(mine, other, out):
    rows = pl.ds(out.shape[0], out.shape[0])
    out[...] = (mine[rows] + other[rows].astype(jnp.float32)).astype(out.dtype)


def partner_sum(mine, other):
    return pl.pallas_call(
        sum_kernel,
        out_shape=jax.ShapeDtypeStruct((mine.shape[0] // 2, mine.shape[1]), other.dtype),
        in_specs=[VMEM] * 2,
        out_specs=VMEM,
        compiler_params=pltpu.CompilerParams(vmem_limit_bytes=SMALL),
        cost_estimate=pl.CostEstimate(flops=32_768, bytes_accessed=300_000, transcendentals=0),
    )(mine, other)


def last_kernel(mine, other, theirs, weight, out):
    rows = pl.ds(0, out.shape[0])
    sums = mine[rows] + other[rows].astype(jnp.float32) + theirs[...].astype(jnp.float32)
    product = jnp.dot(sums.astype(jnp.bfloat16), weight[...], preferred_element_type=jnp.float32)
    out[...] = jnp.maximum(product, 0.0).astype(out.dtype)


def last(mine, other, theirs, weight):
    return pl.pallas_call(
        last_kernel,
        out_shape=jax.ShapeDtypeStruct(theirs.shape, jnp.bfloat16),
        in_specs=[VMEM] * 4,
        out_specs=VMEM,
        compiler_params=pltpu.CompilerParams(vmem_limit_bytes=SMALL),
        cost_estimate=pl.CostEstimate(flops=17_000_000, bytes_accessed=400_000, transcendentals=0),
    )(mine, other, theirs, weight)


def pairs(features, weight, tile_values, tile_coords, tile_counts):
    planes = lax.axis_size("loop") // 4
    mine, other, theirs = spread(features, planes, tile_counts, tile_coords.T, tile_values)
    return last(mine, other, theirs, weight)


def solution(mesh):
    placed = (
        P(AXES, None),
        P(),
        P(AXES, None, None),
        P(AXES, None),
        P(AXES, None),
    )
    local = pairs if dict(mesh.shape) == {"loop": 16, "rep": 2} else ring
    return jax.shard_map(local, mesh=mesh, in_specs=placed, out_specs=P(AXES, None), check_vma=False)
```

```python
import functools

import jax
import jax.numpy as jnp
from jax import lax
from jax.experimental import pallas as pl
from jax.experimental.pallas import tpu as pltpu
from jax.sharding import PartitionSpec as P

AXES = ("loop", "rep")
VMEM = pl.BlockSpec(memory_space=pltpu.VMEM)
SMEM = pl.BlockSpec(memory_space=pltpu.SMEM)


def from_behind(x, axis, by):
    count = lax.axis_size(axis)
    return lax.ppermute(x, axis, [(i, (i + by) % count) for i in range(count)])


def ring(features, weight, tile_values, tile_coords, tile_counts):
    rep_size = lax.axis_size("rep")
    loop_size = lax.axis_size("loop")
    step_count = loop_size // rep_size
    tile_size = tile_values.shape[1]
    feat_width = features.shape[1]
    slot_count = tile_values.shape[0] // step_count
    current_slab = lax.all_gather(features, "rep", axis=0, tiled=True)
    block_count = current_slab.shape[0] // tile_size
    values = tile_values.reshape(step_count, slot_count, tile_size, tile_size)
    coords = tile_coords.reshape(step_count, slot_count, 2)
    counts = tile_counts.reshape(step_count)
    rep_rank = lax.axis_index("rep")
    for bit_index in range(rep_size.bit_length() - 1):
        shifted = from_behind(current_slab, "loop", step_count * (1 << bit_index))
        current_slab = jnp.where(rep_rank >> bit_index & 1 == 1, shifted, current_slab)
    running = jnp.zeros((block_count, tile_size, feat_width), jnp.float32)
    for step_index in range(step_count):
        slab_blocks = current_slab.reshape(block_count, tile_size, feat_width)
        pieces = jnp.take(slab_blocks, coords[step_index, :, 1], axis=0)
        products = jnp.einsum(
            "ktc,kcf->ktf", values[step_index], pieces, preferred_element_type=jnp.float32
        )
        live_slot = (jnp.arange(slot_count) < counts[step_index]).astype(jnp.float32)
        running = running.at[coords[step_index, :, 0]].add(products * live_slot[:, None, None])
        if step_index + 1 < step_count:
            current_slab = from_behind(current_slab, "loop", 1)
    summed = lax.psum_scatter(
        running.reshape(block_count * tile_size, feat_width), "rep", scatter_dimension=0, tiled=True
    )
    aggregated = summed.astype(jnp.bfloat16)
    product = jnp.dot(aggregated, weight, preferred_element_type=jnp.float32)
    return jnp.maximum(product, 0.0).astype(jnp.bfloat16)

HELD = 11
SMALL = 4 * 1024 * 1024
MIDDLE = 24 * 1024 * 1024


def route(planes, move):
    pairs = []
    for z in range(planes):
        for x in range(2):
            for core in range(2):
                for y in range(2):
                    z2, x2, core2, y2 = move(z, x, core, y)
                    pairs.append((((z * 2 + x) * 2 + core) * 2 + y, (((z2 % planes) * 2 + x2) * 2 + core2) * 2 + y2))
    return pairs


def pick_kernel(even, odd, *refs):
    out = refs[-1]
    near = (lax.axis_index("loop") >> 1 & 1) == lax.axis_index("rep")
    for chosen, which in ((jnp.logical_not(near), even), (near, odd)):

        @pl.when(chosen)
        def _(which=which):
            start = 0
            for j in which:
                rows = refs[j].shape[0]
                out[pl.ds(start, rows)] = refs[j][...]
                start += rows


def pick(even, odd, *blocks):
    width = blocks[0].shape[1]
    rows = sum(blocks[j].shape[0] for j in even)
    return pl.pallas_call(
        functools.partial(pick_kernel, even, odd),
        out_shape=jax.ShapeDtypeStruct((rows, width), blocks[0].dtype),
        in_specs=[VMEM] * len(blocks),
        out_specs=VMEM,
        compiler_params=pltpu.CompilerParams(vmem_limit_bytes=SMALL),
        cost_estimate=pl.CostEstimate(flops=0, bytes_accessed=200_000, transcendentals=0),
    )(*blocks)


def pair_kernel(value, mate, mark, matrix, both, own):
    core = lax.axis_index("loop") & 1
    rows = value.shape[0]
    both[pl.ds(pl.multiple_of(core * rows, rows), rows)] = value[...]
    both[pl.ds(pl.multiple_of((1 - core) * rows, rows), rows)] = mate[...]
    own[...] = value[...]


def pair(value, mate, mark, matrix):
    rows, width = value.shape
    return pl.pallas_call(
        pair_kernel,
        out_shape=[jax.ShapeDtypeStruct((n * rows, width), value.dtype) for n in (2, 1)],
        in_specs=[VMEM] * 4,
        out_specs=[VMEM] * 2,
        compiler_params=pltpu.CompilerParams(vmem_limit_bytes=SMALL),
        cost_estimate=pl.CostEstimate(flops=0, bytes_accessed=200_000, transcendentals=0),
    )(value, mate, mark, matrix)


def pause_kernel(out):
    out[...] = jnp.zeros_like(out)


def pause(cost):
    return pl.pallas_call(
        pause_kernel,
        out_shape=jax.ShapeDtypeStruct((16, 128), jnp.bfloat16),
        out_specs=VMEM,
        compiler_params=pltpu.CompilerParams(vmem_limit_bytes=SMALL),
        cost_estimate=pl.CostEstimate(flops=cost, bytes_accessed=4096, transcendentals=0),
    )()


def mark_kernel(*refs):
    refs[-1][...] = refs[0][pl.ds(0, 16), pl.ds(0, 128)]


def mark(cost, *values):
    return pl.pallas_call(
        mark_kernel,
        out_shape=jax.ShapeDtypeStruct((16, 128), values[0].dtype),
        in_specs=[VMEM] * len(values),
        out_specs=VMEM,
        compiler_params=pltpu.CompilerParams(vmem_limit_bytes=SMALL),
        cost_estimate=pl.CostEstimate(flops=cost, bytes_accessed=4096, transcendentals=0),
    )(*values)


def spread(features, planes, counts, coords, tile_values):
    def send(value, move):
        return lax.ppermute(value, AXES, route(planes, move))

    def sign(y):
        return 1 if y else -1

    def core(z, x, c, y):
        return z, x, 1 - c, y

    behind = send(features, lambda z, x, c, y: (z + sign(y), x, c, y))
    far = send(features, lambda z, x, c, y: (z + 2, x, c, y))
    mate = send(features, core)
    kept, given = dense(pause(1_000_000_000), counts, coords, tile_values)
    taken = send(given, core)
    both, own = pair(features, mate, mark(500_000_000, behind), kept)
    ahead = send(both, lambda z, x, c, y: (z - sign(y), x, c, y) if c else (z, x, c, 1 - y))
    ready = mark(40_000_000_000, far)
    done = mark(1, taken)
    along_y = send(pick((0, 1), (0, 1), behind, far, done, ready), lambda z, x, c, y: (z, x, c, 1 - y))
    across = send(pick((0, 1), (1, 2), own, behind, far, done, ready), lambda z, x, c, y: (z, 1 - x, c, 1 - y))
    along_x = send(pick((1,), (0,), own, far, done, ready), lambda z, x, c, y: (z, 1 - x, c, y))
    beside = send(ahead, lambda z, x, c, y: (z, 1 - x, c, y) if c else (z, x, c, y))
    arrived = mark(4_000_000_000, along_y, across, along_x)
    held = [own, far, along_y, across, along_x, ahead, beside]
    other = send(products(1, taken, held, arrived, jnp.bfloat16), core)
    theirs = partner_sum(products(1, kept, held, arrived, jnp.float32), other)
    theirs = send(theirs, lambda z, x, c, y: (z, x, c, 1 - y))
    other = send(products(0, taken, held, arrived, jnp.float32), core)
    mine = products(0, kept, held, arrived, jnp.float32)
    return mine, other, theirs, mark(2_000_000_000, theirs)


def dense_kernel(mark, counts, coords, values, kept, given, total):
    steps = counts.shape[1]
    slots = values.shape[0] // steps
    tile = values.shape[1]
    core = lax.axis_index("loop") & 1
    rank = lax.axis_index("rep")
    near = (lax.axis_index("loop") >> 1 & 1) == rank
    kept[...] = jnp.zeros_like(kept)
    given[...] = jnp.zeros_like(given)

    def one(step, carry):
        total[...] = jnp.zeros_like(total)

        def add(slot, carry):
            row = coords[0, step * slots + slot] ^ rank
            column = coords[1, step * slots + slot] ^ rank
            spot = row * 2 + column
            total[spot] = total[spot] + values[step * slots + slot].astype(jnp.float32)
            return carry

        lax.fori_loop(0, counts[0, step], add, 0)
        odd = step & 1
        there = odd * (1 - 2 * core)
        k = jnp.where(rank == 0, step + there, steps - step - there) >> 1
        half = k >> 1
        parity = core ^ odd
        turned = k & 1 == 1
        paired = (k == 1) == near
        straight = jnp.where(k == 2, 7 + parity, half >> 1)
        homes = (
            jnp.where(jnp.where(turned, paired, k == 2), 1, parity),
            jnp.where(k == 0, 0, parity),
        )
        places = (
            jnp.where(turned, jnp.where(paired, 9 + parity, 6), straight),
            jnp.where(turned, 4 + half, jnp.where(k == 0, 7 + parity, 1 + half)),
        )
        for column in range(2):
            start = pl.multiple_of(places[column] * tile, tile)
            for out, here in ((kept, homes[column] == core), (given, homes[column] != core)):

                @pl.when(here)
                def _(out=out, column=column, start=start):
                    for row in range(2):
                        piece = total[row * 2 + column].astype(jnp.bfloat16)
                        out[pl.ds(row * tile, tile), pl.ds(start, tile)] = piece

        return carry

    lax.fori_loop(0, steps, one, 0)


def dense(mark, tile_counts, tile_coords, tile_values):
    tile = tile_values.shape[1]
    return pl.pallas_call(
        dense_kernel,
        out_shape=[jax.ShapeDtypeStruct((2 * tile, HELD * tile), jnp.bfloat16)] * 2,
        in_specs=[VMEM, SMEM, SMEM, VMEM],
        out_specs=[VMEM, VMEM],
        scratch_shapes=[pltpu.VMEM((4, tile, tile), jnp.float32)],
        compiler_params=pltpu.CompilerParams(vmem_limit_bytes=MIDDLE),
        cost_estimate=pl.CostEstimate(flops=1, bytes_accessed=1, transcendentals=0),
    )(mark, tile_counts, tile_coords, tile_values)


def product_kernel(first, matrix, mark, *refs):
    out = refs[-1]
    span = pl.ds(first, out.shape[0])
    total = jnp.zeros(out.shape, jnp.float32)
    groups = [refs[:2]] + [[ref] for ref in refs[2:4]] + [refs[4:5]] + [[ref] for ref in refs[5:-1]]
    start = 0
    for group in groups:
        rows = jnp.concatenate([ref[...] for ref in group])
        depth = rows.shape[0]
        total += jnp.dot(matrix[span, pl.ds(start, depth)], rows, preferred_element_type=jnp.float32)
        start += depth
    out[...] = total.astype(out.dtype)


def products(half, matrix, blocks, mark, dtype):
    rows = matrix.shape[0] // 2
    width = blocks[0].shape[1]
    return pl.pallas_call(
        functools.partial(product_kernel, half * rows),
        out_shape=jax.ShapeDtypeStruct((rows, width), dtype),
        in_specs=[VMEM] * (2 + len(blocks)),
        out_specs=VMEM,
        compiler_params=pltpu.CompilerParams(vmem_limit_bytes=MIDDLE),
        cost_estimate=pl.CostEstimate(flops=84_000_000, bytes_accessed=1_000_000, transcendentals=0),
    )(matrix, mark, *blocks)


def sum_kernel(mine, other, out):
    out[...] = (mine[...] + other[...].astype(jnp.float32)).astype(out.dtype)


def partner_sum(mine, other):
    return pl.pallas_call(
        sum_kernel,
        out_shape=jax.ShapeDtypeStruct(other.shape, other.dtype),
        in_specs=[VMEM] * 2,
        out_specs=VMEM,
        compiler_params=pltpu.CompilerParams(vmem_limit_bytes=SMALL),
        cost_estimate=pl.CostEstimate(flops=32_768, bytes_accessed=300_000, transcendentals=0),
    )(mine, other)


def last_kernel(theirs, mine, other, weight, mark, out):
    sums = mine[...] + other[...] + theirs[...].astype(jnp.float32)
    product = jnp.dot(sums.astype(jnp.bfloat16), weight[...], preferred_element_type=jnp.float32)
    out[...] = jnp.maximum(product, 0.0).astype(out.dtype)


def last(mine, other, theirs, weight, mark):
    return pl.pallas_call(
        last_kernel,
        out_shape=jax.ShapeDtypeStruct(theirs.shape, jnp.bfloat16),
        in_specs=[VMEM] * 5,
        out_specs=VMEM,
        compiler_params=pltpu.CompilerParams(vmem_limit_bytes=SMALL),
        cost_estimate=pl.CostEstimate(flops=17_000_000, bytes_accessed=400_000, transcendentals=0),
    )(theirs, mine, other, weight, mark)


def pairs(features, weight, tile_values, tile_coords, tile_counts):
    planes = lax.axis_size("loop") // 4
    mine, other, theirs, arrived = spread(features, planes, tile_counts, tile_coords.T, tile_values)
    return last(mine, other, theirs, weight, arrived)


def solution(mesh):
    placed = (
        P(AXES, None),
        P(),
        P(AXES, None, None),
        P(AXES, None),
        P(AXES, None),
    )
    local = pairs if dict(mesh.shape) == {"loop": 16, "rep": 2} else ring
    return jax.shard_map(local, mesh=mesh, in_specs=placed, out_specs=P(AXES, None), check_vma=False)
```

```python
import functools

import jax
import jax.numpy as jnp
from jax import lax
from jax.experimental import pallas as pl
from jax.experimental.pallas import tpu as pltpu
from jax.sharding import PartitionSpec as P

AXES = ("loop", "rep")
VMEM = pl.BlockSpec(memory_space=pltpu.VMEM)
SMEM = pl.BlockSpec(memory_space=pltpu.SMEM)


def from_behind(x, axis, by):
    count = lax.axis_size(axis)
    return lax.ppermute(x, axis, [(i, (i + by) % count) for i in range(count)])


def ring(features, weight, tile_values, tile_coords, tile_counts):
    rep_size = lax.axis_size("rep")
    loop_size = lax.axis_size("loop")
    step_count = loop_size // rep_size
    tile_size = tile_values.shape[1]
    feat_width = features.shape[1]
    slot_count = tile_values.shape[0] // step_count
    current_slab = lax.all_gather(features, "rep", axis=0, tiled=True)
    block_count = current_slab.shape[0] // tile_size
    values = tile_values.reshape(step_count, slot_count, tile_size, tile_size)
    coords = tile_coords.reshape(step_count, slot_count, 2)
    counts = tile_counts.reshape(step_count)
    rep_rank = lax.axis_index("rep")
    for bit_index in range(rep_size.bit_length() - 1):
        shifted = from_behind(current_slab, "loop", step_count * (1 << bit_index))
        current_slab = jnp.where(rep_rank >> bit_index & 1 == 1, shifted, current_slab)
    running = jnp.zeros((block_count, tile_size, feat_width), jnp.float32)
    for step_index in range(step_count):
        slab_blocks = current_slab.reshape(block_count, tile_size, feat_width)
        pieces = jnp.take(slab_blocks, coords[step_index, :, 1], axis=0)
        products = jnp.einsum(
            "ktc,kcf->ktf", values[step_index], pieces, preferred_element_type=jnp.float32
        )
        live_slot = (jnp.arange(slot_count) < counts[step_index]).astype(jnp.float32)
        running = running.at[coords[step_index, :, 0]].add(products * live_slot[:, None, None])
        if step_index + 1 < step_count:
            current_slab = from_behind(current_slab, "loop", 1)
    summed = lax.psum_scatter(
        running.reshape(block_count * tile_size, feat_width), "rep", scatter_dimension=0, tiled=True
    )
    aggregated = summed.astype(jnp.bfloat16)
    product = jnp.dot(aggregated, weight, preferred_element_type=jnp.float32)
    return jnp.maximum(product, 0.0).astype(jnp.bfloat16)

HELD = 11
SMALL = 4 * 1024 * 1024
MIDDLE = 24 * 1024 * 1024


def route(planes, move):
    pairs = []
    for z in range(planes):
        for x in range(2):
            for core in range(2):
                for y in range(2):
                    z2, x2, core2, y2 = move(z, x, core, y)
                    pairs.append((((z * 2 + x) * 2 + core) * 2 + y, (((z2 % planes) * 2 + x2) * 2 + core2) * 2 + y2))
    return pairs


def pick_kernel(even, odd, *refs):
    out = refs[-1]
    near = (lax.axis_index("loop") >> 1 & 1) == lax.axis_index("rep")
    for chosen, which in ((jnp.logical_not(near), even), (near, odd)):

        @pl.when(chosen)
        def _(which=which):
            start = 0
            for j in which:
                rows = refs[j].shape[0]
                out[pl.ds(start, rows)] = refs[j][...]
                start += rows


def pick(even, odd, *blocks):
    width = blocks[0].shape[1]
    rows = sum(blocks[j].shape[0] for j in even)
    return pl.pallas_call(
        functools.partial(pick_kernel, even, odd),
        out_shape=jax.ShapeDtypeStruct((rows, width), blocks[0].dtype),
        in_specs=[VMEM] * len(blocks),
        out_specs=VMEM,
        compiler_params=pltpu.CompilerParams(vmem_limit_bytes=SMALL),
        cost_estimate=pl.CostEstimate(flops=0, bytes_accessed=200_000, transcendentals=0),
    )(*blocks)


def pair_kernel(value, mate, mark, matrix, both, own):
    core = lax.axis_index("loop") & 1
    rows = value.shape[0]
    both[pl.ds(pl.multiple_of(core * rows, rows), rows)] = value[...]
    both[pl.ds(pl.multiple_of((1 - core) * rows, rows), rows)] = mate[...]
    own[...] = value[...]


def pair(value, mate, mark, matrix):
    rows, width = value.shape
    return pl.pallas_call(
        pair_kernel,
        out_shape=[jax.ShapeDtypeStruct((n * rows, width), value.dtype) for n in (2, 1)],
        in_specs=[VMEM] * 4,
        out_specs=[VMEM] * 2,
        compiler_params=pltpu.CompilerParams(vmem_limit_bytes=SMALL),
        cost_estimate=pl.CostEstimate(flops=0, bytes_accessed=200_000, transcendentals=0),
    )(value, mate, mark, matrix)


def pause_kernel(out):
    out[...] = jnp.zeros_like(out)


def pause(cost):
    return pl.pallas_call(
        pause_kernel,
        out_shape=jax.ShapeDtypeStruct((16, 128), jnp.bfloat16),
        out_specs=VMEM,
        compiler_params=pltpu.CompilerParams(vmem_limit_bytes=SMALL),
        cost_estimate=pl.CostEstimate(flops=cost, bytes_accessed=4096, transcendentals=0),
    )()


def mark_kernel(*refs):
    refs[-1][...] = refs[0][pl.ds(0, 16), pl.ds(0, 128)]


def mark(cost, *values):
    return pl.pallas_call(
        mark_kernel,
        out_shape=jax.ShapeDtypeStruct((16, 128), values[0].dtype),
        in_specs=[VMEM] * len(values),
        out_specs=VMEM,
        compiler_params=pltpu.CompilerParams(vmem_limit_bytes=SMALL),
        cost_estimate=pl.CostEstimate(flops=cost, bytes_accessed=4096, transcendentals=0),
    )(*values)


def spread(features, planes, counts, coords, tile_values):
    def send(value, move):
        return lax.ppermute(value, AXES, route(planes, move))

    def sign(y):
        return 1 if y else -1

    def core(z, x, c, y):
        return z, x, 1 - c, y

    behind = send(features, lambda z, x, c, y: (z + sign(y), x, c, y))
    far = send(features, lambda z, x, c, y: (z + 2, x, c, y))
    mate = send(features, core)
    kept, given = dense(pause(1_000_000_000), counts, coords, tile_values)
    taken = send(given, core)
    both, own = pair(features, mate, mark(500_000_000, behind), kept)
    ahead = send(both, lambda z, x, c, y: (z - sign(y), x, c, y) if c else (z, x, c, 1 - y))
    ready = mark(40_000_000_000, far)
    done = mark(1, taken)
    along_y = send(pick((0, 1), (0, 1), behind, far, done, ready), lambda z, x, c, y: (z, x, c, 1 - y))
    across = send(pick((0, 1), (1, 2), own, behind, far, done, ready), lambda z, x, c, y: (z, 1 - x, c, 1 - y))
    along_x = send(pick((1,), (0,), own, far, done, ready), lambda z, x, c, y: (z, 1 - x, c, y))
    beside = send(ahead, lambda z, x, c, y: (z, 1 - x, c, y) if c else (z, x, c, y))
    arrived = mark(4_000_000_000, along_y, across, along_x)
    held = [own, far, along_y, across, along_x, ahead, beside]
    crossing = send(products(1, kept, held, arrived, jnp.bfloat16), core)
    theirs = partner_sum(products(1, taken, held, arrived, jnp.float32), crossing)
    theirs = send(theirs, lambda z, x, c, y: (z, x, 1 - c, 1 - y))
    other = send(products(0, taken, held, arrived, jnp.float32), core)
    mine = products(0, kept, held, arrived, jnp.float32)
    return mine, other, theirs, mark(2_000_000_000, theirs)


def dense_kernel(mark, counts, coords, values, kept, given, total):
    steps = counts.shape[1]
    slots = values.shape[0] // steps
    tile = values.shape[1]
    core = lax.axis_index("loop") & 1
    rank = lax.axis_index("rep")
    near = (lax.axis_index("loop") >> 1 & 1) == rank
    kept[...] = jnp.zeros_like(kept)
    given[...] = jnp.zeros_like(given)

    def one(step):
        total[...] = jnp.zeros_like(total)

        def add(slot, carry):
            row = coords[0, step * slots + slot] ^ rank
            column = coords[1, step * slots + slot] ^ rank
            spot = row * 2 + column
            total[spot] = total[spot] + values[step * slots + slot].astype(jnp.float32)
            return carry

        lax.fori_loop(0, counts[0, step], add, 0)
        odd = step & 1
        there = odd * (1 - 2 * core)
        k = jnp.where(rank == 0, step + there, steps - step - there) >> 1
        half = k >> 1
        parity = core ^ odd
        turned = k & 1 == 1
        paired = (k == 1) == near
        straight = jnp.where(k == 2, 7 + parity, half >> 1)
        homes = (
            jnp.where(jnp.where(turned, paired, k == 2), 1, parity),
            jnp.where(k == 0, 0, parity),
        )
        places = (
            jnp.where(turned, jnp.where(paired, 9 + parity, 6), straight),
            jnp.where(turned, 4 + half, jnp.where(k == 0, 7 + parity, 1 + half)),
        )
        for column in range(2):
            start = pl.multiple_of(places[column] * tile, tile)
            for out, here in ((kept, homes[column] == core), (given, homes[column] != core)):

                @pl.when(here)
                def _(out=out, column=column, start=start):
                    for row in range(2):
                        piece = total[row * 2 + column].astype(jnp.bfloat16)
                        out[pl.ds(row * tile, tile), pl.ds(start, tile)] = piece

    for step in range(steps):
        one(step)


def dense(mark, tile_counts, tile_coords, tile_values):
    tile = tile_values.shape[1]
    return pl.pallas_call(
        dense_kernel,
        out_shape=[jax.ShapeDtypeStruct((2 * tile, HELD * tile), jnp.bfloat16)] * 2,
        in_specs=[VMEM, SMEM, SMEM, VMEM],
        out_specs=[VMEM, VMEM],
        scratch_shapes=[pltpu.VMEM((4, tile, tile), jnp.float32)],
        compiler_params=pltpu.CompilerParams(vmem_limit_bytes=MIDDLE),
        cost_estimate=pl.CostEstimate(flops=1, bytes_accessed=1, transcendentals=0),
    )(mark, tile_counts, tile_coords, tile_values)


def dots(matrix, rows, blocks):
    total = jnp.zeros((rows.size, blocks[0].shape[1]), jnp.float32)
    start = 0
    for block in blocks:
        depth = block.shape[0]
        total += jnp.dot(matrix[rows, pl.ds(start, depth)], block[...], preferred_element_type=jnp.float32)
        start += depth
    return total


def product_kernel(first, matrix, mark, *refs):
    out = refs[-1]
    rows = pl.ds(first, out.shape[0])
    total = jnp.zeros(out.shape, jnp.float32)
    start = 0
    for block in refs[:-1]:
        depth = block.shape[0]
        total += jnp.dot(matrix[rows, pl.ds(start, depth)], block[...], preferred_element_type=jnp.float32)
        start += depth
    out[...] = total.astype(out.dtype)


def products(half, matrix, blocks, mark, dtype):
    rows = matrix.shape[0] // 2
    width = blocks[0].shape[1]
    return pl.pallas_call(
        functools.partial(product_kernel, half * rows),
        out_shape=jax.ShapeDtypeStruct((rows, width), dtype),
        in_specs=[VMEM] * (2 + len(blocks)),
        out_specs=VMEM,
        compiler_params=pltpu.CompilerParams(vmem_limit_bytes=MIDDLE),
        cost_estimate=pl.CostEstimate(flops=84_000_000, bytes_accessed=1_000_000, transcendentals=0),
    )(matrix, mark, *blocks)


def sum_kernel(mine, other, out):
    out[...] = (mine[...] + other[...].astype(jnp.float32)).astype(out.dtype)


def partner_sum(mine, other):
    return pl.pallas_call(
        sum_kernel,
        out_shape=jax.ShapeDtypeStruct(mine.shape, other.dtype),
        in_specs=[VMEM] * 2,
        out_specs=VMEM,
        compiler_params=pltpu.CompilerParams(vmem_limit_bytes=SMALL),
        cost_estimate=pl.CostEstimate(flops=32_768, bytes_accessed=300_000, transcendentals=0),
    )(mine, other)


def last_kernel(theirs, mine, other, weight, mark, out):
    sums = mine[...] + other[...] + theirs[...].astype(jnp.float32)
    product = jnp.dot(sums.astype(jnp.bfloat16), weight[...], preferred_element_type=jnp.float32)
    out[...] = jnp.maximum(product, 0.0).astype(out.dtype)


def last(mine, other, theirs, weight, mark):
    return pl.pallas_call(
        last_kernel,
        out_shape=jax.ShapeDtypeStruct(theirs.shape, jnp.bfloat16),
        in_specs=[VMEM] * 5,
        out_specs=VMEM,
        compiler_params=pltpu.CompilerParams(vmem_limit_bytes=SMALL),
        cost_estimate=pl.CostEstimate(flops=17_000_000, bytes_accessed=400_000, transcendentals=0),
    )(theirs, mine, other, weight, mark)


def pairs(features, weight, tile_values, tile_coords, tile_counts):
    planes = lax.axis_size("loop") // 4
    mine, other, theirs, late = spread(features, planes, tile_counts, tile_coords.T, tile_values)
    return last(mine, other, theirs, weight, late)


def solution(mesh):
    placed = (
        P(AXES, None),
        P(),
        P(AXES, None, None),
        P(AXES, None),
        P(AXES, None),
    )
    local = pairs if dict(mesh.shape) == {"loop": 16, "rep": 2} else ring
    return jax.shard_map(local, mesh=mesh, in_specs=placed, out_specs=P(AXES, None), check_vma=False)
```

```python
import functools

import jax
import jax.numpy as jnp
from jax import lax
from jax.experimental import pallas as pl
from jax.experimental.pallas import tpu as pltpu
from jax.sharding import PartitionSpec as P

AXES = ("loop", "rep")
VMEM = pl.BlockSpec(memory_space=pltpu.VMEM)
SMEM = pl.BlockSpec(memory_space=pltpu.SMEM)


def from_behind(x, axis, by):
    count = lax.axis_size(axis)
    return lax.ppermute(x, axis, [(i, (i + by) % count) for i in range(count)])


def ring(features, weight, tile_values, tile_coords, tile_counts):
    rep_size = lax.axis_size("rep")
    loop_size = lax.axis_size("loop")
    step_count = loop_size // rep_size
    tile_size = tile_values.shape[1]
    feat_width = features.shape[1]
    slot_count = tile_values.shape[0] // step_count
    current_slab = lax.all_gather(features, "rep", axis=0, tiled=True)
    block_count = current_slab.shape[0] // tile_size
    values = tile_values.reshape(step_count, slot_count, tile_size, tile_size)
    coords = tile_coords.reshape(step_count, slot_count, 2)
    counts = tile_counts.reshape(step_count)
    rep_rank = lax.axis_index("rep")
    for bit_index in range(rep_size.bit_length() - 1):
        shifted = from_behind(current_slab, "loop", step_count * (1 << bit_index))
        current_slab = jnp.where(rep_rank >> bit_index & 1 == 1, shifted, current_slab)
    running = jnp.zeros((block_count, tile_size, feat_width), jnp.float32)
    for step_index in range(step_count):
        slab_blocks = current_slab.reshape(block_count, tile_size, feat_width)
        pieces = jnp.take(slab_blocks, coords[step_index, :, 1], axis=0)
        products = jnp.einsum(
            "ktc,kcf->ktf", values[step_index], pieces, preferred_element_type=jnp.float32
        )
        live_slot = (jnp.arange(slot_count) < counts[step_index]).astype(jnp.float32)
        running = running.at[coords[step_index, :, 0]].add(products * live_slot[:, None, None])
        if step_index + 1 < step_count:
            current_slab = from_behind(current_slab, "loop", 1)
    summed = lax.psum_scatter(
        running.reshape(block_count * tile_size, feat_width), "rep", scatter_dimension=0, tiled=True
    )
    aggregated = summed.astype(jnp.bfloat16)
    product = jnp.dot(aggregated, weight, preferred_element_type=jnp.float32)
    return jnp.maximum(product, 0.0).astype(jnp.bfloat16)

HELD = 11
SMALL = 4 * 1024 * 1024
MIDDLE = 24 * 1024 * 1024


def route(planes, move):
    pairs = []
    for z in range(planes):
        for x in range(2):
            for core in range(2):
                for y in range(2):
                    z2, x2, core2, y2 = move(z, x, core, y)
                    pairs.append((((z * 2 + x) * 2 + core) * 2 + y, (((z2 % planes) * 2 + x2) * 2 + core2) * 2 + y2))
    return pairs


def pick_kernel(even, odd, *refs):
    out = refs[-1]
    near = (lax.axis_index("loop") >> 1 & 1) == lax.axis_index("rep")
    for chosen, which in ((jnp.logical_not(near), even), (near, odd)):

        @pl.when(chosen)
        def _(which=which):
            start = 0
            for j in which:
                rows = refs[j].shape[0]
                out[pl.ds(start, rows)] = refs[j][...]
                start += rows


def pick(even, odd, *blocks):
    width = blocks[0].shape[1]
    rows = sum(blocks[j].shape[0] for j in even)
    return pl.pallas_call(
        functools.partial(pick_kernel, even, odd),
        out_shape=jax.ShapeDtypeStruct((rows, width), blocks[0].dtype),
        in_specs=[VMEM] * len(blocks),
        out_specs=VMEM,
        compiler_params=pltpu.CompilerParams(vmem_limit_bytes=SMALL),
        cost_estimate=pl.CostEstimate(flops=0, bytes_accessed=200_000, transcendentals=0),
    )(*blocks)


def pair_kernel(value, mate, mark, matrix, both, own):
    core = lax.axis_index("loop") & 1
    rows = value.shape[0]
    both[pl.ds(pl.multiple_of(core * rows, rows), rows)] = value[...]
    both[pl.ds(pl.multiple_of((1 - core) * rows, rows), rows)] = mate[...]
    own[...] = value[...]


def pair(value, mate, mark, matrix):
    rows, width = value.shape
    return pl.pallas_call(
        pair_kernel,
        out_shape=[jax.ShapeDtypeStruct((n * rows, width), value.dtype) for n in (2, 1)],
        in_specs=[VMEM] * 4,
        out_specs=[VMEM] * 2,
        compiler_params=pltpu.CompilerParams(vmem_limit_bytes=SMALL),
        cost_estimate=pl.CostEstimate(flops=0, bytes_accessed=200_000, transcendentals=0),
    )(value, mate, mark, matrix)


def pause_kernel(out):
    out[...] = jnp.zeros_like(out)


def pause(cost):
    return pl.pallas_call(
        pause_kernel,
        out_shape=jax.ShapeDtypeStruct((16, 128), jnp.bfloat16),
        out_specs=VMEM,
        compiler_params=pltpu.CompilerParams(vmem_limit_bytes=SMALL),
        cost_estimate=pl.CostEstimate(flops=cost, bytes_accessed=4096, transcendentals=0),
    )()


def mark_kernel(*refs):
    refs[-1][...] = refs[0][pl.ds(0, 16), pl.ds(0, 128)]


def mark(cost, *values):
    return pl.pallas_call(
        mark_kernel,
        out_shape=jax.ShapeDtypeStruct((16, 128), values[0].dtype),
        in_specs=[VMEM] * len(values),
        out_specs=VMEM,
        compiler_params=pltpu.CompilerParams(vmem_limit_bytes=SMALL),
        cost_estimate=pl.CostEstimate(flops=cost, bytes_accessed=4096, transcendentals=0),
    )(*values)


def spread(features, planes, counts, coords, tile_values):
    def send(value, move):
        return lax.ppermute(value, AXES, route(planes, move))

    def sign(y):
        return 1 if y else -1

    def core(z, x, c, y):
        return z, x, 1 - c, y

    behind = send(features, lambda z, x, c, y: (z + sign(y), x, c, y))
    far = send(features, lambda z, x, c, y: (z + 2, x, c, y))
    mate = send(features, core)
    kept, given = dense(pause(1_000_000_000), counts, coords, tile_values)
    taken = send(given, core)
    both, own = pair(features, mate, mark(500_000_000, behind), kept)
    ahead = send(both, lambda z, x, c, y: (z - sign(y), x, c, y) if c else (z, x, c, 1 - y))
    ready = mark(40_000_000_000, far)
    done = mark(1, taken)
    along_y = send(pick((0, 1), (0, 1), behind, far, done, ready), lambda z, x, c, y: (z, x, c, 1 - y))
    across = send(pick((0, 1), (1, 2), own, behind, far, done, ready), lambda z, x, c, y: (z, 1 - x, c, 1 - y))
    along_x = send(pick((1,), (0,), own, far, done, ready), lambda z, x, c, y: (z, 1 - x, c, y))
    beside = send(ahead, lambda z, x, c, y: (z, 1 - x, c, y) if c else (z, x, c, y))
    arrived = mark(4_000_000_000, along_y, across, along_x)
    held = [own, far, along_y, across, along_x, ahead, beside]
    crossing = send(products(1, kept, held, arrived, jnp.bfloat16), core)
    theirs = partner_sum(products(1, taken, held, arrived, jnp.float32), crossing)
    theirs = send(theirs, lambda z, x, c, y: (z, x, 1 - c, 1 - y))
    other = send(products(0, taken, held, arrived, jnp.float32), core)
    mine = products(0, kept, held, arrived, jnp.float32)
    return mine, other, theirs, mark(2_000_000_000, theirs)


def dense_kernel(mark, counts, coords, values, kept, given, total):
    steps = counts.shape[1]
    slots = values.shape[0] // steps
    tile = values.shape[1]
    core = lax.axis_index("loop") & 1
    rank = lax.axis_index("rep")
    near = (lax.axis_index("loop") >> 1 & 1) == rank
    kept[...] = jnp.zeros_like(kept)
    given[...] = jnp.zeros_like(given)

    def one(step):
        for spot in range(4):
            total[spot] = jnp.zeros_like(total[spot])

        def add(group, carry):
            for i in range(3):
                slot = group * 3 + i
                row = coords[0, step * slots + slot] ^ rank
                column = coords[1, step * slots + slot] ^ rank
                spot = jnp.where(slot < counts[0, step], row * 2 + column, 4)
                total[spot] = total[spot] + values[step * slots + slot].astype(jnp.float32)
            return carry

        lax.fori_loop(0, (counts[0, step] + 2) // 3, add, 0)
        odd = step & 1
        there = odd * (1 - 2 * core)
        k = jnp.where(rank == 0, step + there, steps - step - there) >> 1
        half = k >> 1
        parity = core ^ odd
        turned = k & 1 == 1
        paired = (k == 1) == near
        straight = jnp.where(k == 2, 7 + parity, half >> 1)
        homes = (
            jnp.where(jnp.where(turned, paired, k == 2), 1, parity),
            jnp.where(k == 0, 0, parity),
        )
        places = (
            jnp.where(turned, jnp.where(paired, 9 + parity, 6), straight),
            jnp.where(turned, 4 + half, jnp.where(k == 0, 7 + parity, 1 + half)),
        )
        for column in range(2):
            start = pl.multiple_of(places[column] * tile, tile)
            for out, here in ((kept, homes[column] == core), (given, homes[column] != core)):

                @pl.when(here)
                def _(out=out, column=column, start=start):
                    for row in range(2):
                        piece = total[row * 2 + column].astype(jnp.bfloat16)
                        out[pl.ds(row * tile, tile), pl.ds(start, tile)] = piece

    for step in range(steps):
        one(step)


def dense(mark, tile_counts, tile_coords, tile_values):
    tile = tile_values.shape[1]
    return pl.pallas_call(
        dense_kernel,
        out_shape=[jax.ShapeDtypeStruct((2 * tile, HELD * tile), jnp.bfloat16)] * 2,
        in_specs=[VMEM, SMEM, SMEM, VMEM],
        out_specs=[VMEM, VMEM],
        scratch_shapes=[pltpu.VMEM((5, tile, tile), jnp.float32)],
        compiler_params=pltpu.CompilerParams(vmem_limit_bytes=MIDDLE),
        cost_estimate=pl.CostEstimate(flops=1, bytes_accessed=1, transcendentals=0),
    )(mark, tile_counts, tile_coords, tile_values)


def dots(matrix, rows, blocks):
    total = jnp.zeros((rows.size, blocks[0].shape[1]), jnp.float32)
    start = 0
    for block in blocks:
        depth = block.shape[0]
        total += jnp.dot(matrix[rows, pl.ds(start, depth)], block[...], preferred_element_type=jnp.float32)
        start += depth
    return total


def product_kernel(first, matrix, mark, *refs):
    out = refs[-1]
    rows = pl.ds(first, out.shape[0])
    total = jnp.zeros(out.shape, jnp.float32)
    start = 0
    for block in refs[:-1]:
        depth = block.shape[0]
        total += jnp.dot(matrix[rows, pl.ds(start, depth)], block[...], preferred_element_type=jnp.float32)
        start += depth
    out[...] = total.astype(out.dtype)


def products(half, matrix, blocks, mark, dtype):
    rows = matrix.shape[0] // 2
    width = blocks[0].shape[1]
    return pl.pallas_call(
        functools.partial(product_kernel, half * rows),
        out_shape=jax.ShapeDtypeStruct((rows, width), dtype),
        in_specs=[VMEM] * (2 + len(blocks)),
        out_specs=VMEM,
        compiler_params=pltpu.CompilerParams(vmem_limit_bytes=MIDDLE),
        cost_estimate=pl.CostEstimate(flops=84_000_000, bytes_accessed=1_000_000, transcendentals=0),
    )(matrix, mark, *blocks)


def sum_kernel(mine, other, out):
    out[...] = (mine[...] + other[...].astype(jnp.float32)).astype(out.dtype)


def partner_sum(mine, other):
    return pl.pallas_call(
        sum_kernel,
        out_shape=jax.ShapeDtypeStruct(mine.shape, other.dtype),
        in_specs=[VMEM] * 2,
        out_specs=VMEM,
        compiler_params=pltpu.CompilerParams(vmem_limit_bytes=SMALL),
        cost_estimate=pl.CostEstimate(flops=32_768, bytes_accessed=300_000, transcendentals=0),
    )(mine, other)


def last_kernel(theirs, mine, other, weight, mark, out):
    sums = mine[...] + other[...] + theirs[...].astype(jnp.float32)
    product = jnp.dot(sums.astype(jnp.bfloat16), weight[...], preferred_element_type=jnp.float32)
    out[...] = jnp.maximum(product, 0.0).astype(out.dtype)


def last(mine, other, theirs, weight, mark):
    return pl.pallas_call(
        last_kernel,
        out_shape=jax.ShapeDtypeStruct(theirs.shape, jnp.bfloat16),
        in_specs=[VMEM] * 5,
        out_specs=VMEM,
        compiler_params=pltpu.CompilerParams(vmem_limit_bytes=SMALL),
        cost_estimate=pl.CostEstimate(flops=17_000_000, bytes_accessed=400_000, transcendentals=0),
    )(theirs, mine, other, weight, mark)


def pairs(features, weight, tile_values, tile_coords, tile_counts):
    planes = lax.axis_size("loop") // 4
    mine, other, theirs, late = spread(features, planes, tile_counts, tile_coords.T, tile_values)
    return last(mine, other, theirs, weight, late)


def solution(mesh):
    placed = (
        P(AXES, None),
        P(),
        P(AXES, None, None),
        P(AXES, None),
        P(AXES, None),
    )
    local = pairs if dict(mesh.shape) == {"loop": 16, "rep": 2} else ring
    return jax.shard_map(local, mesh=mesh, in_specs=placed, out_specs=P(AXES, None), check_vma=False)
```

```python
import functools

import jax
import jax.numpy as jnp
from jax import lax
from jax.experimental import pallas as pl
from jax.experimental.pallas import tpu as pltpu
from jax.sharding import PartitionSpec as P

AXES = ("loop", "rep")
VMEM = pl.BlockSpec(memory_space=pltpu.VMEM)
SMEM = pl.BlockSpec(memory_space=pltpu.SMEM)


def from_behind(x, axis, by):
    count = lax.axis_size(axis)
    return lax.ppermute(x, axis, [(i, (i + by) % count) for i in range(count)])


def ring(features, weight, tile_values, tile_coords, tile_counts):
    rep_size = lax.axis_size("rep")
    loop_size = lax.axis_size("loop")
    step_count = loop_size // rep_size
    tile_size = tile_values.shape[1]
    feat_width = features.shape[1]
    slot_count = tile_values.shape[0] // step_count
    current_slab = lax.all_gather(features, "rep", axis=0, tiled=True)
    block_count = current_slab.shape[0] // tile_size
    values = tile_values.reshape(step_count, slot_count, tile_size, tile_size)
    coords = tile_coords.reshape(step_count, slot_count, 2)
    counts = tile_counts.reshape(step_count)
    rep_rank = lax.axis_index("rep")
    for bit_index in range(rep_size.bit_length() - 1):
        shifted = from_behind(current_slab, "loop", step_count * (1 << bit_index))
        current_slab = jnp.where(rep_rank >> bit_index & 1 == 1, shifted, current_slab)
    running = jnp.zeros((block_count, tile_size, feat_width), jnp.float32)
    for step_index in range(step_count):
        slab_blocks = current_slab.reshape(block_count, tile_size, feat_width)
        pieces = jnp.take(slab_blocks, coords[step_index, :, 1], axis=0)
        products = jnp.einsum(
            "ktc,kcf->ktf", values[step_index], pieces, preferred_element_type=jnp.float32
        )
        live_slot = (jnp.arange(slot_count) < counts[step_index]).astype(jnp.float32)
        running = running.at[coords[step_index, :, 0]].add(products * live_slot[:, None, None])
        if step_index + 1 < step_count:
            current_slab = from_behind(current_slab, "loop", 1)
    summed = lax.psum_scatter(
        running.reshape(block_count * tile_size, feat_width), "rep", scatter_dimension=0, tiled=True
    )
    aggregated = summed.astype(jnp.bfloat16)
    product = jnp.dot(aggregated, weight, preferred_element_type=jnp.float32)
    return jnp.maximum(product, 0.0).astype(jnp.bfloat16)

HELD = 11
SMALL = 4 * 1024 * 1024
MIDDLE = 24 * 1024 * 1024


def route(planes, move):
    pairs = []
    for z in range(planes):
        for x in range(2):
            for core in range(2):
                for y in range(2):
                    z2, x2, core2, y2 = move(z, x, core, y)
                    pairs.append((((z * 2 + x) * 2 + core) * 2 + y, (((z2 % planes) * 2 + x2) * 2 + core2) * 2 + y2))
    return pairs


def pick_kernel(even, odd, *refs):
    out = refs[-1]
    near = (lax.axis_index("loop") >> 1 & 1) == lax.axis_index("rep")
    for chosen, which in ((jnp.logical_not(near), even), (near, odd)):

        @pl.when(chosen)
        def _(which=which):
            start = 0
            for j in which:
                rows = refs[j].shape[0]
                out[pl.ds(start, rows)] = refs[j][...]
                start += rows


def pick(even, odd, *blocks):
    width = blocks[0].shape[1]
    rows = sum(blocks[j].shape[0] for j in even)
    return pl.pallas_call(
        functools.partial(pick_kernel, even, odd),
        out_shape=jax.ShapeDtypeStruct((rows, width), blocks[0].dtype),
        in_specs=[VMEM] * len(blocks),
        out_specs=VMEM,
        compiler_params=pltpu.CompilerParams(vmem_limit_bytes=SMALL),
        cost_estimate=pl.CostEstimate(flops=0, bytes_accessed=200_000, transcendentals=0),
    )(*blocks)


def pair_kernel(value, mate, mark, matrix, both, own):
    core = lax.axis_index("loop") & 1
    rows = value.shape[0]
    both[pl.ds(pl.multiple_of(core * rows, rows), rows)] = value[...]
    both[pl.ds(pl.multiple_of((1 - core) * rows, rows), rows)] = mate[...]
    own[...] = value[...]


def pair(value, mate, mark, matrix):
    rows, width = value.shape
    return pl.pallas_call(
        pair_kernel,
        out_shape=[jax.ShapeDtypeStruct((n * rows, width), value.dtype) for n in (2, 1)],
        in_specs=[VMEM] * 4,
        out_specs=[VMEM] * 2,
        compiler_params=pltpu.CompilerParams(vmem_limit_bytes=SMALL),
        cost_estimate=pl.CostEstimate(flops=0, bytes_accessed=200_000, transcendentals=0),
    )(value, mate, mark, matrix)


def pause_kernel(out):
    out[...] = jnp.zeros_like(out)


def pause(cost):
    return pl.pallas_call(
        pause_kernel,
        out_shape=jax.ShapeDtypeStruct((16, 128), jnp.bfloat16),
        out_specs=VMEM,
        compiler_params=pltpu.CompilerParams(vmem_limit_bytes=SMALL),
        cost_estimate=pl.CostEstimate(flops=cost, bytes_accessed=4096, transcendentals=0),
    )()


def mark_kernel(*refs):
    refs[-1][...] = refs[0][pl.ds(0, 16), pl.ds(0, 128)]


def mark(cost, *values):
    return pl.pallas_call(
        mark_kernel,
        out_shape=jax.ShapeDtypeStruct((16, 128), values[0].dtype),
        in_specs=[VMEM] * len(values),
        out_specs=VMEM,
        compiler_params=pltpu.CompilerParams(vmem_limit_bytes=SMALL),
        cost_estimate=pl.CostEstimate(flops=cost, bytes_accessed=4096, transcendentals=0),
    )(*values)


def spread(features, planes, counts, coords, tile_values):
    def send(value, move):
        return lax.ppermute(value, AXES, route(planes, move))

    def sign(y):
        return 1 if y else -1

    def core(z, x, c, y):
        return z, x, 1 - c, y

    behind = send(features, lambda z, x, c, y: (z + sign(y), x, c, y))
    far = send(features, lambda z, x, c, y: (z + 2, x, c, y))
    mate = send(features, core)
    kept, given = dense(pause(1_000_000_000), counts, coords, tile_values)
    taken = send(given, core)
    both, own = pair(features, mate, mark(500_000_000, behind), kept)
    ahead = send(both, lambda z, x, c, y: (z - sign(y), x, c, y) if c else (z, x, c, 1 - y))
    ready = mark(40_000_000_000, far)
    done = mark(1, taken)
    along_y = send(pick((0, 1), (0, 1), behind, far, done, ready), lambda z, x, c, y: (z, x, c, 1 - y))
    across = send(pick((0, 1), (1, 2), own, behind, far, done, ready), lambda z, x, c, y: (z, 1 - x, c, 1 - y))
    along_x = send(pick((1,), (0,), own, far, done, ready), lambda z, x, c, y: (z, 1 - x, c, y))
    beside = send(ahead, lambda z, x, c, y: (z, 1 - x, c, y) if c else (z, x, c, y))
    kept_sums, taken_sums = early_products(far, own, ahead, kept, taken)
    arrived = mark(4_000_000_000, along_y, across, along_x, kept_sums)
    late = [along_y, across, along_x, beside]
    held = [own, far, along_y, across, along_x, ahead, beside]
    crossing = send(late_products(kept, kept_sums, late, arrived, jnp.bfloat16), core)
    theirs = partner_sum(late_products(taken, taken_sums, late, arrived, jnp.float32), crossing)
    theirs = send(theirs, lambda z, x, c, y: (z, x, 1 - c, 1 - y))
    other = send(products(taken, held, arrived), core)
    mine = products(kept, held, arrived)
    return mine, other, theirs, mark(2_000_000_000, theirs)


def dense_kernel(mark, counts, coords, values, kept, given, total):
    steps = counts.shape[1]
    slots = values.shape[0] // steps
    tile = values.shape[1]
    core = lax.axis_index("loop") & 1
    rank = lax.axis_index("rep")
    near = (lax.axis_index("loop") >> 1 & 1) == rank
    for out in (kept, given):
        for first, count in ((0, 2), (3, 1), (7, 4)):
            span = pl.ds(first * tile, count * tile)
            out[:, span] = jnp.zeros((2 * tile, count * tile), out.dtype)

    def one(step):
        for spot in range(4):
            total[spot] = jnp.zeros_like(total[spot])

        def add(group, carry):
            for i in range(3):
                slot = group * 3 + i
                row = coords[0, step * slots + slot] ^ rank
                column = coords[1, step * slots + slot] ^ rank
                spot = jnp.where(slot < counts[0, step], row * 2 + column, 4)
                total[spot] = total[spot] + values[step * slots + slot].astype(jnp.float32)
            return carry

        lax.fori_loop(0, (counts[0, step] + 2) // 3, add, 0)
        odd = step & 1
        there = odd * (1 - 2 * core)
        k = jnp.where(rank == 0, step + there, steps - step - there) >> 1
        half = k >> 1
        parity = core ^ odd
        turned = k & 1 == 1
        paired = (k == 1) == near
        straight = jnp.where(k == 2, 7 + parity, half >> 1)
        homes = (
            jnp.where(jnp.where(turned, paired, k == 2), 1, parity),
            jnp.where(k == 0, 0, parity),
        )
        places = (
            jnp.where(turned, jnp.where(paired, 9 + parity, 6), straight),
            jnp.where(turned, 4 + half, jnp.where(k == 0, 7 + parity, 1 + half)),
        )
        for column in range(2):
            start = pl.multiple_of(places[column] * tile, tile)
            for out, here in ((kept, homes[column] == core), (given, homes[column] != core)):

                @pl.when(here)
                def _(out=out, column=column, start=start):
                    for row in range(2):
                        piece = total[row * 2 + column].astype(jnp.bfloat16)
                        out[pl.ds(row * tile, tile), pl.ds(start, tile)] = piece

    for step in range(steps):
        one(step)


def dense(mark, tile_counts, tile_coords, tile_values):
    tile = tile_values.shape[1]
    return pl.pallas_call(
        dense_kernel,
        out_shape=[jax.ShapeDtypeStruct((2 * tile, HELD * tile), jnp.bfloat16)] * 2,
        in_specs=[VMEM, SMEM, SMEM, VMEM],
        out_specs=[VMEM, VMEM],
        scratch_shapes=[pltpu.VMEM((5, tile, tile), jnp.float32)],
        compiler_params=pltpu.CompilerParams(vmem_limit_bytes=MIDDLE),
        cost_estimate=pl.CostEstimate(flops=1, bytes_accessed=1, transcendentals=0),
    )(mark, tile_counts, tile_coords, tile_values)


def dots(matrix, rows, blocks):
    total = jnp.zeros((rows.size, blocks[0].shape[1]), jnp.float32)
    start = 0
    for block in blocks:
        depth = block.shape[0]
        total += jnp.dot(matrix[rows, pl.ds(start, depth)], block[...], preferred_element_type=jnp.float32)
        start += depth
    return total


def dots(matrix, rows, starts, blocks, total):
    for start, block in zip(starts, blocks, strict=True):
        part = matrix[rows, pl.ds(start * rows.size, block.shape[0])]
        total += jnp.dot(part, block[...], preferred_element_type=jnp.float32)
    return total


def early_kernel(far, own, ahead, kept, taken, *outs):
    for matrix, out in zip((kept, taken), outs, strict=True):
        rows = pl.ds(out.shape[0], out.shape[0])
        out[...] = dots(matrix, rows, (0, 1, 7), (own, far, ahead), jnp.zeros(out.shape, jnp.float32))


def early_products(far, own, ahead, kept, taken):
    return pl.pallas_call(
        early_kernel,
        out_shape=[jax.ShapeDtypeStruct((kept.shape[0] // 2, own.shape[1]), jnp.float32)] * 2,
        in_specs=[VMEM] * 5,
        out_specs=[VMEM] * 2,
        compiler_params=pltpu.CompilerParams(vmem_limit_bytes=MIDDLE),
        cost_estimate=pl.CostEstimate(flops=1, bytes_accessed=1, transcendentals=0),
    )(far, own, ahead, kept, taken)


def late_kernel(matrix, mark, sums, *refs):
    out = refs[-1]
    rows = pl.ds(out.shape[0], out.shape[0])
    out[...] = dots(matrix, rows, (2, 4, 6, 9), refs[:-1], sums[...]).astype(out.dtype)


def late_products(matrix, sums, blocks, mark, dtype):
    return pl.pallas_call(
        late_kernel,
        out_shape=jax.ShapeDtypeStruct(sums.shape, dtype),
        in_specs=[VMEM] * (3 + len(blocks)),
        out_specs=VMEM,
        compiler_params=pltpu.CompilerParams(vmem_limit_bytes=MIDDLE),
        cost_estimate=pl.CostEstimate(flops=54_000_000, bytes_accessed=700_000, transcendentals=0),
    )(matrix, mark, sums, *blocks)


def product_kernel(matrix, mark, *refs):
    out = refs[-1]
    rows = pl.ds(0, out.shape[0])
    starts = (0, 1, 2, 4, 6, 7, 9)
    out[...] = dots(matrix, rows, starts, refs[:-1], jnp.zeros(out.shape, jnp.float32))


def products(matrix, blocks, mark):
    rows = matrix.shape[0] // 2
    width = blocks[0].shape[1]
    return pl.pallas_call(
        product_kernel,
        out_shape=jax.ShapeDtypeStruct((rows, width), jnp.float32),
        in_specs=[VMEM] * (2 + len(blocks)),
        out_specs=VMEM,
        compiler_params=pltpu.CompilerParams(vmem_limit_bytes=MIDDLE),
        cost_estimate=pl.CostEstimate(flops=84_000_000, bytes_accessed=1_000_000, transcendentals=0),
    )(matrix, mark, *blocks)


def sum_kernel(mine, other, out):
    out[...] = (mine[...] + other[...].astype(jnp.float32)).astype(out.dtype)


def partner_sum(mine, other):
    return pl.pallas_call(
        sum_kernel,
        out_shape=jax.ShapeDtypeStruct(mine.shape, other.dtype),
        in_specs=[VMEM] * 2,
        out_specs=VMEM,
        compiler_params=pltpu.CompilerParams(vmem_limit_bytes=SMALL),
        cost_estimate=pl.CostEstimate(flops=32_768, bytes_accessed=300_000, transcendentals=0),
    )(mine, other)


def last_kernel(theirs, mine, other, weight, mark, out):
    sums = mine[...] + other[...] + theirs[...].astype(jnp.float32)
    product = jnp.dot(sums.astype(jnp.bfloat16), weight[...], preferred_element_type=jnp.float32)
    out[...] = jnp.maximum(product, 0.0).astype(out.dtype)


def last(mine, other, theirs, weight, mark):
    return pl.pallas_call(
        last_kernel,
        out_shape=jax.ShapeDtypeStruct(theirs.shape, jnp.bfloat16),
        in_specs=[VMEM] * 5,
        out_specs=VMEM,
        compiler_params=pltpu.CompilerParams(vmem_limit_bytes=SMALL),
        cost_estimate=pl.CostEstimate(flops=17_000_000, bytes_accessed=400_000, transcendentals=0),
    )(theirs, mine, other, weight, mark)


def pairs(features, weight, tile_values, tile_coords, tile_counts):
    planes = lax.axis_size("loop") // 4
    mine, other, theirs, late = spread(features, planes, tile_counts, tile_coords.T, tile_values)
    return last(mine, other, theirs, weight, late)


def solution(mesh):
    placed = (
        P(AXES, None),
        P(),
        P(AXES, None, None),
        P(AXES, None),
        P(AXES, None),
    )
    local = pairs if dict(mesh.shape) == {"loop": 16, "rep": 2} else ring
    return jax.shard_map(local, mesh=mesh, in_specs=placed, out_specs=P(AXES, None), check_vma=False)
```

```python
import functools

import jax
import jax.numpy as jnp
from jax import lax
from jax.experimental import pallas as pl
from jax.experimental.pallas import tpu as pltpu
from jax.sharding import PartitionSpec as P

AXES = ("loop", "rep")
VMEM = pl.BlockSpec(memory_space=pltpu.VMEM)
SMEM = pl.BlockSpec(memory_space=pltpu.SMEM)


def from_behind(x, axis, by):
    count = lax.axis_size(axis)
    return lax.ppermute(x, axis, [(i, (i + by) % count) for i in range(count)])


def ring(features, weight, tile_values, tile_coords, tile_counts):
    rep_size = lax.axis_size("rep")
    loop_size = lax.axis_size("loop")
    step_count = loop_size // rep_size
    tile_size = tile_values.shape[1]
    feat_width = features.shape[1]
    slot_count = tile_values.shape[0] // step_count
    current_slab = lax.all_gather(features, "rep", axis=0, tiled=True)
    block_count = current_slab.shape[0] // tile_size
    values = tile_values.reshape(step_count, slot_count, tile_size, tile_size)
    coords = tile_coords.reshape(step_count, slot_count, 2)
    counts = tile_counts.reshape(step_count)
    rep_rank = lax.axis_index("rep")
    for bit_index in range(rep_size.bit_length() - 1):
        shifted = from_behind(current_slab, "loop", step_count * (1 << bit_index))
        current_slab = jnp.where(rep_rank >> bit_index & 1 == 1, shifted, current_slab)
    running = jnp.zeros((block_count, tile_size, feat_width), jnp.float32)
    for step_index in range(step_count):
        slab_blocks = current_slab.reshape(block_count, tile_size, feat_width)
        pieces = jnp.take(slab_blocks, coords[step_index, :, 1], axis=0)
        products = jnp.einsum(
            "ktc,kcf->ktf", values[step_index], pieces, preferred_element_type=jnp.float32
        )
        live_slot = (jnp.arange(slot_count) < counts[step_index]).astype(jnp.float32)
        running = running.at[coords[step_index, :, 0]].add(products * live_slot[:, None, None])
        if step_index + 1 < step_count:
            current_slab = from_behind(current_slab, "loop", 1)
    summed = lax.psum_scatter(
        running.reshape(block_count * tile_size, feat_width), "rep", scatter_dimension=0, tiled=True
    )
    aggregated = summed.astype(jnp.bfloat16)
    product = jnp.dot(aggregated, weight, preferred_element_type=jnp.float32)
    return jnp.maximum(product, 0.0).astype(jnp.bfloat16)

HELD = 11
SMALL = 4 * 1024 * 1024
MIDDLE = 24 * 1024 * 1024


def route(planes, move):
    pairs = []
    for z in range(planes):
        for x in range(2):
            for core in range(2):
                for y in range(2):
                    z2, x2, core2, y2 = move(z, x, core, y)
                    pairs.append((((z * 2 + x) * 2 + core) * 2 + y, (((z2 % planes) * 2 + x2) * 2 + core2) * 2 + y2))
    return pairs


def pick_kernel(even, odd, *refs):
    out = refs[-1]
    near = (lax.axis_index("loop") >> 1 & 1) == lax.axis_index("rep")
    for chosen, which in ((jnp.logical_not(near), even), (near, odd)):

        @pl.when(chosen)
        def _(which=which):
            start = 0
            for j in which:
                rows = refs[j].shape[0]
                out[pl.ds(start, rows)] = refs[j][...]
                start += rows


def pick(even, odd, *blocks):
    width = blocks[0].shape[1]
    rows = sum(blocks[j].shape[0] for j in even)
    return pl.pallas_call(
        functools.partial(pick_kernel, even, odd),
        out_shape=jax.ShapeDtypeStruct((rows, width), blocks[0].dtype),
        in_specs=[VMEM] * len(blocks),
        out_specs=VMEM,
        compiler_params=pltpu.CompilerParams(vmem_limit_bytes=SMALL),
        cost_estimate=pl.CostEstimate(flops=0, bytes_accessed=200_000, transcendentals=0),
    )(*blocks)


def pair_kernel(value, mate, mark, matrix, both, own):
    core = lax.axis_index("loop") & 1
    rows = value.shape[0]
    both[pl.ds(pl.multiple_of(core * rows, rows), rows)] = value[...]
    both[pl.ds(pl.multiple_of((1 - core) * rows, rows), rows)] = mate[...]
    own[...] = value[...]


def pair(value, mate, mark, matrix):
    rows, width = value.shape
    return pl.pallas_call(
        pair_kernel,
        out_shape=[jax.ShapeDtypeStruct((n * rows, width), value.dtype) for n in (2, 1)],
        in_specs=[VMEM] * 4,
        out_specs=[VMEM] * 2,
        compiler_params=pltpu.CompilerParams(vmem_limit_bytes=SMALL),
        cost_estimate=pl.CostEstimate(flops=0, bytes_accessed=200_000, transcendentals=0),
    )(value, mate, mark, matrix)


def pause_kernel(out):
    out[...] = jnp.zeros_like(out)


def pause(cost):
    return pl.pallas_call(
        pause_kernel,
        out_shape=jax.ShapeDtypeStruct((16, 128), jnp.bfloat16),
        out_specs=VMEM,
        compiler_params=pltpu.CompilerParams(vmem_limit_bytes=SMALL),
        cost_estimate=pl.CostEstimate(flops=cost, bytes_accessed=4096, transcendentals=0),
    )()


def mark_kernel(*refs):
    refs[-1][...] = refs[0][pl.ds(0, 16), pl.ds(0, 128)]


def mark(cost, *values):
    return pl.pallas_call(
        mark_kernel,
        out_shape=jax.ShapeDtypeStruct((16, 128), values[0].dtype),
        in_specs=[VMEM] * len(values),
        out_specs=VMEM,
        compiler_params=pltpu.CompilerParams(vmem_limit_bytes=SMALL),
        cost_estimate=pl.CostEstimate(flops=cost, bytes_accessed=4096, transcendentals=0),
    )(*values)


def spread(features, planes, counts, coords, tile_values):
    def send(value, move):
        return lax.ppermute(value, AXES, route(planes, move))

    def sign(y):
        return 1 if y else -1

    def core(z, x, c, y):
        return z, x, 1 - c, y

    behind = send(features, lambda z, x, c, y: (z + sign(y), x, c, y))
    far = send(features, lambda z, x, c, y: (z + 2, x, c, y))
    mate = send(features, core)
    kept, given = dense(pause(1_000_000_000), counts, coords, tile_values)
    taken = send(given, core)
    both, own = pair(features, mate, mark(500_000_000, behind), kept)
    ahead = send(both, lambda z, x, c, y: (z - sign(y), x, c, y) if c else (z, x, c, 1 - y))
    ready = mark(40_000_000_000, far)
    done = mark(1, taken)
    along_y = send(pick((0, 1), (0, 1), behind, far, done, ready), lambda z, x, c, y: (z, x, c, 1 - y))
    across = send(pick((0, 1), (1, 2), own, behind, far, done, ready), lambda z, x, c, y: (z, 1 - x, c, 1 - y))
    along_x = send(pick((1,), (0,), own, far, done, ready), lambda z, x, c, y: (z, 1 - x, c, y))
    beside = send(ahead, lambda z, x, c, y: (z, 1 - x, c, y) if c else (z, x, c, y))
    arrived = mark(4_000_000_000, along_y, across, along_x)
    held = [own, far, along_y, across, along_x, ahead, beside]
    crossing = send(products(1, kept, held, arrived, jnp.bfloat16), core)
    theirs = partner_sum(products(1, taken, held, arrived, jnp.float32), crossing)
    theirs = send(theirs, lambda z, x, c, y: (z, x, 1 - c, 1 - y))
    other = send(products(0, taken, held, arrived, jnp.float32), core)
    mine = products(0, kept, held, arrived, jnp.float32)
    return mine, other, theirs, mark(2_000_000_000, theirs)


def dense_kernel(mark, counts, coords, values, kept, given, total):
    steps = counts.shape[1]
    slots = values.shape[0] // steps
    tile = values.shape[1]
    core = lax.axis_index("loop") & 1
    rank = lax.axis_index("rep")
    near = (lax.axis_index("loop") >> 1 & 1) == rank
    for out in (kept, given):
        for first, count in ((0, 2), (3, 1), (7, 4)):
            span = pl.ds(first * tile, count * tile)
            out[:, span] = jnp.zeros((2 * tile, count * tile), out.dtype)

    def one(step):
        for spot in range(4):
            total[spot] = jnp.zeros_like(total[spot])

        def add(group, carry):
            for i in range(4):
                slot = group * 4 + i
                row = coords[0, step * slots + slot] ^ rank
                column = coords[1, step * slots + slot] ^ rank
                spot = jnp.where(slot < counts[0, step], row * 2 + column, 4)
                total[spot] = total[spot] + values[step * slots + slot].astype(jnp.float32)
            return carry

        lax.fori_loop(0, (counts[0, step] + 3) // 4, add, 0)
        odd = step & 1
        there = odd * (1 - 2 * core)
        k = jnp.where(rank == 0, step + there, steps - step - there) >> 1
        half = k >> 1
        parity = core ^ odd
        turned = k & 1 == 1
        paired = (k == 1) == near
        straight = jnp.where(k == 2, 7 + parity, half >> 1)
        homes = (
            jnp.where(jnp.where(turned, paired, k == 2), 1, parity),
            jnp.where(k == 0, 0, parity),
        )
        places = (
            jnp.where(turned, jnp.where(paired, 9 + parity, 6), straight),
            jnp.where(turned, 4 + half, jnp.where(k == 0, 7 + parity, 1 + half)),
        )
        for column in range(2):
            start = pl.multiple_of(places[column] * tile, tile)
            for out, here in ((kept, homes[column] == core), (given, homes[column] != core)):

                @pl.when(here)
                def _(out=out, column=column, start=start):
                    for row in range(2):
                        piece = total[row * 2 + column].astype(jnp.bfloat16)
                        out[pl.ds(row * tile, tile), pl.ds(start, tile)] = piece

    for step in range(steps):
        one(step)


def dense(mark, tile_counts, tile_coords, tile_values):
    tile = tile_values.shape[1]
    return pl.pallas_call(
        dense_kernel,
        out_shape=[jax.ShapeDtypeStruct((2 * tile, HELD * tile), jnp.bfloat16)] * 2,
        in_specs=[VMEM, SMEM, SMEM, VMEM],
        out_specs=[VMEM, VMEM],
        scratch_shapes=[pltpu.VMEM((5, tile, tile), jnp.float32)],
        compiler_params=pltpu.CompilerParams(vmem_limit_bytes=MIDDLE),
        cost_estimate=pl.CostEstimate(flops=1, bytes_accessed=1, transcendentals=0),
    )(mark, tile_counts, tile_coords, tile_values)


def dots(matrix, rows, blocks):
    total = jnp.zeros((rows.size, blocks[0].shape[1]), jnp.float32)
    start = 0
    for block in blocks:
        depth = block.shape[0]
        total += jnp.dot(matrix[rows, pl.ds(start, depth)], block[...], preferred_element_type=jnp.float32)
        start += depth
    return total


def product_kernel(first, matrix, mark, *refs):
    out = refs[-1]
    rows = pl.ds(first, out.shape[0])
    total = jnp.zeros(out.shape, jnp.float32)
    start = 0
    for block in refs[:-1]:
        depth = block.shape[0]
        total += jnp.dot(matrix[rows, pl.ds(start, depth)], block[...], preferred_element_type=jnp.float32)
        start += depth
    out[...] = total.astype(out.dtype)


def products(half, matrix, blocks, mark, dtype):
    rows = matrix.shape[0] // 2
    width = blocks[0].shape[1]
    return pl.pallas_call(
        functools.partial(product_kernel, half * rows),
        out_shape=jax.ShapeDtypeStruct((rows, width), dtype),
        in_specs=[VMEM] * (2 + len(blocks)),
        out_specs=VMEM,
        compiler_params=pltpu.CompilerParams(vmem_limit_bytes=MIDDLE),
        cost_estimate=pl.CostEstimate(flops=84_000_000, bytes_accessed=1_000_000, transcendentals=0),
    )(matrix, mark, *blocks)


def sum_kernel(mine, other, out):
    out[...] = (mine[...] + other[...].astype(jnp.float32)).astype(out.dtype)


def partner_sum(mine, other):
    return pl.pallas_call(
        sum_kernel,
        out_shape=jax.ShapeDtypeStruct(mine.shape, other.dtype),
        in_specs=[VMEM] * 2,
        out_specs=VMEM,
        compiler_params=pltpu.CompilerParams(vmem_limit_bytes=SMALL),
        cost_estimate=pl.CostEstimate(flops=32_768, bytes_accessed=300_000, transcendentals=0),
    )(mine, other)


def last_kernel(theirs, mine, other, weight, mark, out):
    sums = mine[...] + other[...] + theirs[...].astype(jnp.float32)
    product = jnp.dot(sums.astype(jnp.bfloat16), weight[...], preferred_element_type=jnp.float32)
    out[...] = jnp.maximum(product, 0.0).astype(out.dtype)


def last(mine, other, theirs, weight, mark):
    return pl.pallas_call(
        last_kernel,
        out_shape=jax.ShapeDtypeStruct(theirs.shape, jnp.bfloat16),
        in_specs=[VMEM] * 5,
        out_specs=VMEM,
        compiler_params=pltpu.CompilerParams(vmem_limit_bytes=SMALL),
        cost_estimate=pl.CostEstimate(flops=17_000_000, bytes_accessed=400_000, transcendentals=0),
    )(theirs, mine, other, weight, mark)


def pairs(features, weight, tile_values, tile_coords, tile_counts):
    planes = lax.axis_size("loop") // 4
    mine, other, theirs, late = spread(features, planes, tile_counts, tile_coords.T, tile_values)
    return last(mine, other, theirs, weight, late)


def solution(mesh):
    placed = (
        P(AXES, None),
        P(),
        P(AXES, None, None),
        P(AXES, None),
        P(AXES, None),
    )
    local = pairs if dict(mesh.shape) == {"loop": 16, "rep": 2} else ring
    return jax.shard_map(local, mesh=mesh, in_specs=placed, out_specs=P(AXES, None), check_vma=False)
```

```python
import functools

import jax
import jax.numpy as jnp
from jax import lax
from jax.experimental import pallas as pl
from jax.experimental.pallas import tpu as pltpu
from jax.sharding import PartitionSpec as P

AXES = ("loop", "rep")
VMEM = pl.BlockSpec(memory_space=pltpu.VMEM)
SMEM = pl.BlockSpec(memory_space=pltpu.SMEM)


def from_behind(x, axis, by):
    count = lax.axis_size(axis)
    return lax.ppermute(x, axis, [(i, (i + by) % count) for i in range(count)])


def ring(features, weight, tile_values, tile_coords, tile_counts):
    rep_size = lax.axis_size("rep")
    loop_size = lax.axis_size("loop")
    step_count = loop_size // rep_size
    tile_size = tile_values.shape[1]
    feat_width = features.shape[1]
    slot_count = tile_values.shape[0] // step_count
    current_slab = lax.all_gather(features, "rep", axis=0, tiled=True)
    block_count = current_slab.shape[0] // tile_size
    values = tile_values.reshape(step_count, slot_count, tile_size, tile_size)
    coords = tile_coords.reshape(step_count, slot_count, 2)
    counts = tile_counts.reshape(step_count)
    rep_rank = lax.axis_index("rep")
    for bit_index in range(rep_size.bit_length() - 1):
        shifted = from_behind(current_slab, "loop", step_count * (1 << bit_index))
        current_slab = jnp.where(rep_rank >> bit_index & 1 == 1, shifted, current_slab)
    running = jnp.zeros((block_count, tile_size, feat_width), jnp.float32)
    for step_index in range(step_count):
        slab_blocks = current_slab.reshape(block_count, tile_size, feat_width)
        pieces = jnp.take(slab_blocks, coords[step_index, :, 1], axis=0)
        products = jnp.einsum(
            "ktc,kcf->ktf", values[step_index], pieces, preferred_element_type=jnp.float32
        )
        live_slot = (jnp.arange(slot_count) < counts[step_index]).astype(jnp.float32)
        running = running.at[coords[step_index, :, 0]].add(products * live_slot[:, None, None])
        if step_index + 1 < step_count:
            current_slab = from_behind(current_slab, "loop", 1)
    summed = lax.psum_scatter(
        running.reshape(block_count * tile_size, feat_width), "rep", scatter_dimension=0, tiled=True
    )
    aggregated = summed.astype(jnp.bfloat16)
    product = jnp.dot(aggregated, weight, preferred_element_type=jnp.float32)
    return jnp.maximum(product, 0.0).astype(jnp.bfloat16)

HELD = 11
SMALL = 4 * 1024 * 1024
MIDDLE = 24 * 1024 * 1024


def route(planes, move):
    pairs = []
    for z in range(planes):
        for x in range(2):
            for core in range(2):
                for y in range(2):
                    z2, x2, core2, y2 = move(z, x, core, y)
                    pairs.append((((z * 2 + x) * 2 + core) * 2 + y, (((z2 % planes) * 2 + x2) * 2 + core2) * 2 + y2))
    return pairs


def pick_kernel(even, odd, *refs):
    out = refs[-1]
    near = (lax.axis_index("loop") >> 1 & 1) == lax.axis_index("rep")
    for chosen, which in ((jnp.logical_not(near), even), (near, odd)):

        @pl.when(chosen)
        def _(which=which):
            start = 0
            for j in which:
                rows = refs[j].shape[0]
                out[pl.ds(start, rows)] = refs[j][...]
                start += rows


def pick(even, odd, *blocks):
    width = blocks[0].shape[1]
    rows = sum(blocks[j].shape[0] for j in even)
    return pl.pallas_call(
        functools.partial(pick_kernel, even, odd),
        out_shape=jax.ShapeDtypeStruct((rows, width), blocks[0].dtype),
        in_specs=[VMEM] * len(blocks),
        out_specs=VMEM,
        compiler_params=pltpu.CompilerParams(vmem_limit_bytes=SMALL),
        cost_estimate=pl.CostEstimate(flops=0, bytes_accessed=200_000, transcendentals=0),
    )(*blocks)


def pair_kernel(value, mate, mark, matrix, both, own):
    core = lax.axis_index("loop") & 1
    rows = value.shape[0]
    both[pl.ds(pl.multiple_of(core * rows, rows), rows)] = value[...]
    both[pl.ds(pl.multiple_of((1 - core) * rows, rows), rows)] = mate[...]
    own[...] = value[...]


def pair(value, mate, mark, matrix):
    rows, width = value.shape
    return pl.pallas_call(
        pair_kernel,
        out_shape=[jax.ShapeDtypeStruct((n * rows, width), value.dtype) for n in (2, 1)],
        in_specs=[VMEM] * 4,
        out_specs=[VMEM] * 2,
        compiler_params=pltpu.CompilerParams(vmem_limit_bytes=SMALL),
        cost_estimate=pl.CostEstimate(flops=0, bytes_accessed=200_000, transcendentals=0),
    )(value, mate, mark, matrix)


def pause_kernel(out):
    out[...] = jnp.zeros_like(out)


def pause(cost):
    return pl.pallas_call(
        pause_kernel,
        out_shape=jax.ShapeDtypeStruct((16, 128), jnp.bfloat16),
        out_specs=VMEM,
        compiler_params=pltpu.CompilerParams(vmem_limit_bytes=SMALL),
        cost_estimate=pl.CostEstimate(flops=cost, bytes_accessed=4096, transcendentals=0),
    )()


def mark_kernel(*refs):
    refs[-1][...] = refs[0][pl.ds(0, 16), pl.ds(0, 128)]


def mark(cost, *values):
    return pl.pallas_call(
        mark_kernel,
        out_shape=jax.ShapeDtypeStruct((16, 128), values[0].dtype),
        in_specs=[VMEM] * len(values),
        out_specs=VMEM,
        compiler_params=pltpu.CompilerParams(vmem_limit_bytes=SMALL),
        cost_estimate=pl.CostEstimate(flops=cost, bytes_accessed=4096, transcendentals=0),
    )(*values)


def spread(features, planes, counts, coords, tile_values):
    def send(value, move):
        return lax.ppermute(value, AXES, route(planes, move))

    def sign(y):
        return 1 if y else -1

    def core(z, x, c, y):
        return z, x, 1 - c, y

    behind = send(features, lambda z, x, c, y: (z + sign(y), x, c, y))
    far = send(features, lambda z, x, c, y: (z + 2, x, c, y))
    mate = send(features, core)
    kept, given = dense(pause(1_000_000_000), counts, coords, tile_values)
    taken = send(given, core)
    both, own = pair(features, mate, mark(500_000_000, behind), kept)
    ahead = send(both, lambda z, x, c, y: (z, x, c, 1 - y) if c else (z - sign(y), x, c, y))
    ready = mark(40_000_000_000, far)
    done = mark(1, taken)
    along_y = send(pick((0, 1), (0, 1), behind, far, done, ready), lambda z, x, c, y: (z, x, c, 1 - y))
    across = send(pick((0, 1), (1, 2), own, behind, far, done, ready), lambda z, x, c, y: (z, 1 - x, c, 1 - y))
    along_x = send(pick((1,), (0,), own, far, done, ready), lambda z, x, c, y: (z, 1 - x, c, y))
    beside = send(ahead, lambda z, x, c, y: (z, x, 0, y) if c else (z, 1 - x, 1, y))
    arrived = mark(4_000_000_000, along_y, across, along_x)
    held = [own, far, along_y, across, along_x, ahead, beside]
    crossing = send(products(1, kept, held, arrived, jnp.bfloat16), core)
    theirs = partner_sum(products(1, taken, held, arrived, jnp.float32), crossing)
    theirs = send(theirs, lambda z, x, c, y: (z, x, 1 - c, 1 - y))
    other = send(products(0, taken, held, arrived, jnp.float32), core)
    mine = products(0, kept, held, arrived, jnp.float32)
    return mine, other, theirs, mark(2_000_000_000, theirs)


def dense_kernel(mark, counts, coords, values, kept, given, total):
    steps = counts.shape[1]
    slots = values.shape[0] // steps
    tile = values.shape[1]
    core = lax.axis_index("loop") & 1
    rank = lax.axis_index("rep")
    near = (lax.axis_index("loop") >> 1 & 1) == rank
    kept[...] = jnp.zeros_like(kept)
    given[...] = jnp.zeros_like(given)

    def one(step):
        for spot in range(4):
            total[spot] = jnp.zeros_like(total[spot])

        def add(group, carry):
            for i in range(3):
                slot = group * 3 + i
                row = coords[0, step * slots + slot] ^ rank
                column = coords[1, step * slots + slot] ^ rank
                spot = jnp.where(slot < counts[0, step], row * 2 + column, 4)
                total[spot] = total[spot] + values[step * slots + slot].astype(jnp.float32)
            return carry

        lax.fori_loop(0, (counts[0, step] + 2) // 3, add, 0)
        odd = step & 1
        there = odd * (1 - 2 * core)
        k = jnp.where(rank == 0, step + there, steps - step - there) >> 1
        half = k >> 1
        parity = core ^ odd
        turned = k & 1 == 1
        paired = (k == 1) == near
        straight = jnp.where(k == 2, 7 + parity, half >> 1)
        homes = (
            jnp.where(turned, jnp.where(paired, 1, parity), jnp.where(k == 2, 0, parity)),
            jnp.where(k == 0, 1, parity),
        )
        places = (
            jnp.where(turned, jnp.where(paired, 9 + parity, 6), straight),
            jnp.where(turned, 4 + half, jnp.where(k == 0, 7 + parity, 1 + half)),
        )
        for column in range(2):
            start = pl.multiple_of(places[column] * tile, tile)
            for out, here in ((kept, homes[column] == core), (given, homes[column] != core)):

                @pl.when(here)
                def _(out=out, column=column, start=start):
                    for row in range(2):
                        piece = total[row * 2 + column].astype(jnp.bfloat16)
                        out[pl.ds(row * tile, tile), pl.ds(start, tile)] = piece

    for step in range(steps):
        one(step)


def dense(mark, tile_counts, tile_coords, tile_values):
    tile = tile_values.shape[1]
    return pl.pallas_call(
        dense_kernel,
        out_shape=[jax.ShapeDtypeStruct((2 * tile, HELD * tile), jnp.bfloat16)] * 2,
        in_specs=[VMEM, SMEM, SMEM, VMEM],
        out_specs=[VMEM, VMEM],
        scratch_shapes=[pltpu.VMEM((5, tile, tile), jnp.float32)],
        compiler_params=pltpu.CompilerParams(vmem_limit_bytes=MIDDLE),
        cost_estimate=pl.CostEstimate(flops=1, bytes_accessed=1, transcendentals=0),
    )(mark, tile_counts, tile_coords, tile_values)


def dots(matrix, rows, blocks):
    total = jnp.zeros((rows.size, blocks[0].shape[1]), jnp.float32)
    start = 0
    for block in blocks:
        depth = block.shape[0]
        total += jnp.dot(matrix[rows, pl.ds(start, depth)], block[...], preferred_element_type=jnp.float32)
        start += depth
    return total


def product_kernel(first, matrix, mark, *refs):
    out = refs[-1]
    rows = pl.ds(first, out.shape[0])
    total = jnp.zeros(out.shape, jnp.float32)
    start = 0
    for block in refs[:-1]:
        depth = block.shape[0]
        total += jnp.dot(matrix[rows, pl.ds(start, depth)], block[...], preferred_element_type=jnp.float32)
        start += depth
    out[...] = total.astype(out.dtype)


def products(half, matrix, blocks, mark, dtype):
    rows = matrix.shape[0] // 2
    width = blocks[0].shape[1]
    return pl.pallas_call(
        functools.partial(product_kernel, half * rows),
        out_shape=jax.ShapeDtypeStruct((rows, width), dtype),
        in_specs=[VMEM] * (2 + len(blocks)),
        out_specs=VMEM,
        compiler_params=pltpu.CompilerParams(vmem_limit_bytes=MIDDLE),
        cost_estimate=pl.CostEstimate(flops=84_000_000, bytes_accessed=1_000_000, transcendentals=0),
    )(matrix, mark, *blocks)


def sum_kernel(mine, other, out):
    out[...] = (mine[...] + other[...].astype(jnp.float32)).astype(out.dtype)


def partner_sum(mine, other):
    return pl.pallas_call(
        sum_kernel,
        out_shape=jax.ShapeDtypeStruct(mine.shape, other.dtype),
        in_specs=[VMEM] * 2,
        out_specs=VMEM,
        compiler_params=pltpu.CompilerParams(vmem_limit_bytes=SMALL),
        cost_estimate=pl.CostEstimate(flops=32_768, bytes_accessed=300_000, transcendentals=0),
    )(mine, other)


def last_kernel(theirs, mine, other, weight, mark, out):
    sums = mine[...] + other[...] + theirs[...].astype(jnp.float32)
    product = jnp.dot(sums.astype(jnp.bfloat16), weight[...], preferred_element_type=jnp.float32)
    out[...] = jnp.maximum(product, 0.0).astype(out.dtype)


def last(mine, other, theirs, weight, mark):
    return pl.pallas_call(
        last_kernel,
        out_shape=jax.ShapeDtypeStruct(theirs.shape, jnp.bfloat16),
        in_specs=[VMEM] * 5,
        out_specs=VMEM,
        compiler_params=pltpu.CompilerParams(vmem_limit_bytes=SMALL),
        cost_estimate=pl.CostEstimate(flops=17_000_000, bytes_accessed=400_000, transcendentals=0),
    )(theirs, mine, other, weight, mark)


def pairs(features, weight, tile_values, tile_coords, tile_counts):
    planes = lax.axis_size("loop") // 4
    mine, other, theirs, late = spread(features, planes, tile_counts, tile_coords.T, tile_values)
    return last(mine, other, theirs, weight, late)


def solution(mesh):
    placed = (
        P(AXES, None),
        P(),
        P(AXES, None, None),
        P(AXES, None),
        P(AXES, None),
    )
    local = pairs if dict(mesh.shape) == {"loop": 16, "rep": 2} else ring
    return jax.shard_map(local, mesh=mesh, in_specs=placed, out_specs=P(AXES, None), check_vma=False)
```
